512 devices in a mesh: dp: 64 (over z, y), tensor: 8 (over x, core).
Axes of the slice: x: 4, y: 8, z: 8, core: 2. Of those that a mesh axis runs over, the one named last changes fastest.
Arguments:
- tokens: bfloat16 [49152, 8192], P('dp', 'tensor'), may hold values from -6 to 6
- base_value_matrix: bfloat16 [8192, 1024], P('tensor'), may hold values from -0.0625 to 0.0625
- adapter_down_factors: bfloat16 [256, 64, 8192], P('dp', None, 'tensor'), may hold values from -0.0625 to 0.0625
- adapter_up_factors: bfloat16 [256, 64, 1024], P('dp', None, 'tensor'), may hold values from -0.75 to 0.75
- adapter_storage_slot: int32 [256], replicated, may hold values from 0 to 255, as said below
- segment_adapter_ids: int32 [384], P('dp'), may hold values from 0 to 255, as said below
- segment_live_count: int32 [64], P('dp'), may hold values from 1 to 6, as said below
Outputs:
- values_out: bfloat16 [49152, 1024], P('dp', 'tensor')
The draws below stay inside these ranges and needn't reach their ends.
Inputs may be any that keep to these rules, and one draw needn't show every extreme that they name: `adapter_storage_slot`: A permutation: every storage slot holds one adapter; slot s lies on index s // 4 of dp. `segment_adapter_ids`: every segment of index i of dp names an adapter stored on index (i + o) mod the size of dp, for some offset o with 0 <= o < 4; the first 4 segments of index i name the 4 offsets, one each, and the first segment never names offset 0; two segments of index i that name the same owner name the same adapter. `segment_live_count`: some index of dp has all 6 segments live.
All inputs are finite; a program needn't handle non-finite values.
Results may differ from the reference program's by a relative error of at most 0.0035.
Values may be sent and summed in bfloat16 or wider, within the bound.
A program may use at most 64 MiB of HBM per device.

```python
import jax
import jax.numpy as jnp
from jax import lax

MODEL_WIDTH = 8192
VALUE_FEATURES = 1024
ADAPTER_RANK = 64
SEG = 128
SEGS_DEV = 6
ADP_DEV = 4
ADAPTER_TOTAL = 256
TOKENS = 49152
N_DP = 64


def slot_table(key):
    return jax.random.permutation(key, ADAPTER_TOTAL).astype(jnp.int32)


def draw_adapter_storage_slot(key, part):
    slots = slot_table(key)
    return slots


def draw_segment_adapter_ids(key, part):
    slots = slot_table(key)
    key = jax.random.fold_in(key, 2)
    within_key, first_key, rest_key = jax.random.split(key, 3)
    window = min(4, SEGS_DEV)
    within = jax.random.randint(within_key, (N_DP, window), 0, ADP_DEV).astype(jnp.int32)
    first_keys = jax.random.split(first_key, N_DP)
    remote = jax.vmap(lambda one_key: jax.random.permutation(one_key, window - 1))(first_keys).astype(jnp.int32) + 1
    first = jnp.concatenate([remote, jnp.zeros((N_DP, 1), jnp.int32)], axis=1)
    rest = jax.random.randint(rest_key, (N_DP, SEGS_DEV - window), 0, window).astype(jnp.int32)
    offsets = jnp.concatenate([first, rest], axis=1)
    device = jnp.arange(N_DP, dtype=jnp.int32)[:, None]
    owners = (device + offsets) % N_DP
    local = jnp.take_along_axis(within, offsets, axis=1)
    stored = owners * ADP_DEV + local
    inverse = jnp.argsort(slots).astype(jnp.int32)
    adapters = inverse[stored]
    return adapters.reshape(-1).astype(jnp.int32)


def draw_segment_live_count(key, part):
    key = jax.random.fold_in(key, 3)
    count_key, full_key = jax.random.split(key)
    counts = jax.random.randint(count_key, (N_DP,), 1, SEGS_DEV + 1)
    filled = jax.random.randint(full_key, (), 0, N_DP)
    counts = jnp.where(jnp.arange(N_DP) == filled, SEGS_DEV, counts)
    return counts.astype(jnp.int32)


def level_of(key, dims, cuts, low, top_value):
    def one(dim, blocks):
        draws = jax.random.uniform(jax.random.fold_in(jax.random.fold_in(key, 6), dim), (blocks,), jnp.float32, low / len(cuts), top_value / len(cuts))
        return jnp.repeat(jnp.exp(draws), dims[dim] // blocks).reshape((-1,) + (1,) * (len(dims) - dim - 1))

    factor_of = one(*cuts[0])
    for cut in cuts[1:]:
        factor_of = factor_of * one(*cut)
    return factor_of


def gaussian(key, shape, deviation, limit, pieces=(), kind=jnp.bfloat16):
    values = jax.random.normal(key, shape, jnp.float32) * deviation
    if len(pieces) > 0:
        values = level_of(key, shape, pieces, -0.22, 0.18) * values
    return jnp.clip(values, min=-limit, max=limit).astype(kind)


def setup_inputs(seed: int = 0) -> dict:
    key_of = jax.random.split(jax.random.key(seed), 8)
    return {
        "tokens": gaussian(key_of[0], (TOKENS, MODEL_WIDTH), 1.0, 6.0, ((0, 64), (1, 8))),
        "base_value_matrix": gaussian(key_of[1], (MODEL_WIDTH, VALUE_FEATURES), MODEL_WIDTH ** -0.5, 0.0625, ((0, 8),)),
        "adapter_down_factors": gaussian(key_of[2], (ADAPTER_TOTAL, ADAPTER_RANK, MODEL_WIDTH), MODEL_WIDTH ** -0.5, 0.0625, ((0, 64), (2, 8))),
        "adapter_up_factors": gaussian(key_of[3], (ADAPTER_TOTAL, ADAPTER_RANK, VALUE_FEATURES), ADAPTER_RANK ** -0.5, 0.75, ((0, 64), (2, 8))),
        "adapter_storage_slot": draw_adapter_storage_slot(jax.random.fold_in(key_of[7], 71), 0),
        "segment_adapter_ids": draw_segment_adapter_ids(jax.random.fold_in(key_of[7], 71), 0),
        "segment_live_count": draw_segment_live_count(jax.random.fold_in(key_of[7], 71), 0),
    }


def reference(tokens, base_value_matrix, adapter_down_factors, adapter_up_factors, adapter_storage_slot, segment_adapter_ids, segment_live_count):
    base = jnp.dot(tokens, base_value_matrix, preferred_element_type=jnp.float32)
    total_segs = segment_adapter_ids.shape[0]
    device_portion = total_segs // N_DP
    seg_index = jnp.arange(total_segs, dtype=jnp.int32)
    live = (seg_index % device_portion) < segment_live_count[seg_index // device_portion]
    slots = adapter_storage_slot[segment_adapter_ids]
    seg_rows = tokens.reshape(total_segs, SEG, MODEL_WIDTH)

    def apply_segment(packed):
        token_rows, storage_slot_index, keep = packed
        down_projected = jnp.dot(token_rows, adapter_down_factors[storage_slot_index].T, preferred_element_type=jnp.float32)
        down_projected_half = down_projected.astype(jnp.bfloat16)
        adapter_update = jnp.dot(down_projected_half, adapter_up_factors[storage_slot_index], preferred_element_type=jnp.float32)
        return adapter_update * keep

    deltas = lax.map(apply_segment, (seg_rows, slots, live.astype(jnp.float32)))
    return (base + deltas.reshape(TOKENS, VALUE_FEATURES)).astype(jnp.bfloat16)
```

```python
import functools

import jax
import jax.numpy as jnp
from jax import lax
from jax.experimental import pallas as pl
from jax.experimental.pallas import tpu as pltpu
from jax.sharding import PartitionSpec as P

MESH = pl.DeviceIdType.MESH
F32 = jnp.float32
BF16 = jnp.bfloat16

RING = 8
SEG = 128
RANK = 64
DIRECT = 32
PIECE = 16
PIECES = (RANK - DIRECT) // PIECE
ORDER = (2, 1, 3, 0)


def nt_dot(a, b):
    return lax.dot_general(a, b, (((1,), (1,)), ((), ())), preferred_element_type=F32)


def twice(a):
    return jnp.concatenate([a, a], axis=0)


def kernel(
    n_dp,
    n_tensor,
    tokens_hbm,
    w_hbm,
    down_hbm,
    up_hbm,
    slot_hbm,
    ids_hbm,
    live_hbm,
    out_ref,
    tok,
    w,
    down,
    up,
    slot,
    ids,
    live,
    req_out,
    req_in,
    a_out,
    a_near,
    a_far,
    relay,
    b_out,
    b_near,
    b_far,
    mine,
    core_out,
    core_in,
    x_out,
    x_in,
    s_mine,
    s_out,
    s_in,
    t_mine,
    t_out,
    t_in,
    acc,
    load_sem,
    req_send,
    req_recv,
    a_send,
    a_recv,
    relay_send,
    relay_recv,
    pass_send,
    pass_recv,
    b_send,
    b_recv,
    core_send,
    core_recv,
    x_send,
    x_recv,
    s_send,
    s_recv,
    t_send,
    t_recv,
):
    me = lax.axis_index("dp")
    t = lax.axis_index("tensor")
    n_chip = n_tensor // 2
    segs = tok.shape[0]
    stored = down.shape[0]

    def dp_at(offset):
        return (lax.rem(me + offset + n_dp, n_dp), t)

    def tensor_at(offset):
        return (me, lax.rem(t + offset, n_tensor))

    other_core = (me, t + 1 - 2 * lax.rem(t, 2))
    row = me // RING * RING
    y = lax.rem(me, RING)
    relay_to = (row + lax.rem(y + 2, RING), t)
    relay_from = (row + lax.rem(y + RING - 2, RING), t)
    pass_to = (lax.rem(row + lax.rem(y + RING - 2, RING) - 3 + n_dp, n_dp), t)
    far_owner = lax.rem(me + 3, n_dp)
    pass_from = (far_owner // RING * RING + lax.rem(lax.rem(far_owner, RING) + 2, RING), t)

    def remote(src, dst, send, recv, device):
        return pltpu.make_async_remote_copy(
            src_ref=src, dst_ref=dst, send_sem=send, recv_sem=recv, device_id=device, device_id_type=MESH
        )

    barrier = pltpu.get_barrier_semaphore()
    peers = [dp_at(o) for o in (1, 2, 3, -1, -2, -3)]
    peers += [relay_to, relay_from, pass_to, pass_from]
    peers += [tensor_at(k) for k in range(1, n_tensor)]
    for peer in peers:
        pl.semaphore_signal(barrier, inc=1, device_id=peer, device_id_type=MESH)

    small = [
        pltpu.make_async_copy(src, dst, load_sem.at[i])
        for i, (src, dst) in enumerate(((slot_hbm, slot), (ids_hbm, ids), (live_hbm, live)))
    ]
    down_load = pltpu.make_async_copy(down_hbm, down, load_sem.at[3])
    up_load = pltpu.make_async_copy(up_hbm, up, load_sem.at[4])
    tok_load = pltpu.make_async_copy(tokens_hbm, tok, load_sem.at[5])
    w_load = []
    for i, k in enumerate(ORDER):
        for half in range(2):
            owner = lax.rem(t + 2 * k, n_tensor)
            if half:
                owner = owner + 1 - 2 * lax.rem(owner, 2)
            columns = pl.ds(pl.multiple_of(owner * 128, 128), 128)
            w_load.append(
                pltpu.make_async_copy(
                    w_hbm.at[:, columns], w.at[i, :, pl.ds(half * 128, 128)], load_sem.at[6 + 2 * i + half]
                )
            )
    for copy in small:
        copy.start()
    down_load.start()
    tok_load.start()
    for copy in w_load:
        copy.start()
    up_load.start()

    for copy in small:
        copy.wait()
    offs, locs = [], []
    for s in range(segs):
        place = slot[ids[s]]
        offs.append(lax.rem(place // stored - me + n_dp, n_dp))
        locs.append(lax.rem(place, stored))
    wanted = []
    for o in range(4):
        found = jnp.int32(0)
        for s in range(4):
            found = jnp.where(offs[s] == o, locs[s], found)
        wanted.append(found)
    far_seg = jnp.int32(0)
    for s in range(4):
        far_seg = jnp.where(offs[s] == 3, s, far_seg)
    live_count = live[0]
    for o in range(1, 4):
        req_out[o - 1] = jnp.full(req_out.shape[1:], wanted[o], jnp.int32)

    pl.semaphore_wait(barrier, len(peers))
    asks = [
        remote(req_out.at[o - 1], req_in.at[o - 1], req_send.at[o - 1], req_recv.at[o - 1], dp_at(o))
        for o in range(1, 4)
    ]
    for copy in asks:
        copy.start()

    core_copies = []

    def base_block(i):
        w_load[2 * i].wait()
        w_load[2 * i + 1].wait()

        def rows(s, carry):
            part = jnp.dot(tok[s], w[i], preferred_element_type=F32)
            mine[i, s] = part[:, :128]
            core_out[i, s] = part[:, 128:]
            return carry

        lax.fori_loop(0, segs, rows, 0)
        copy = remote(core_out.at[i], core_in.at[i], core_send.at[i], core_recv.at[i], other_core)
        copy.start()
        core_copies.append(copy)

    a_copies, relay_copies, b_copies = [], [], []

    def serve(o):
        asks[o - 1].wait_recv()
        pick = jnp.max(req_in[o - 1])
        a_out[o - 1] = down[pick]
        b_out[o - 1] = up[pick]
        dst = a_near.at[o] if o < 3 else a_far
        rows = RANK if o < 3 else DIRECT
        copy = remote(
            a_out.at[o - 1, pl.ds(0, rows)], dst.at[pl.ds(0, rows)], a_send.at[o - 1], a_recv.at[o - 1], dp_at(-o)
        )
        copy.start()
        a_copies.append(copy)
        if o == 3:
            for j in range(PIECES):
                copy = remote(
                    a_out.at[o - 1, pl.ds(DIRECT + j * PIECE, PIECE)],
                    relay.at[j],
                    relay_send.at[j],
                    relay_recv.at[j],
                    relay_to,
                )
                copy.start()
                relay_copies.append(copy)

    tok_load.wait()
    base_block(0)
    down_load.wait()
    up_load.wait()
    a_near[0] = down[wanted[0]]
    b_near[0] = twice(up[wanted[0]])
    base_block(1)
    serve(1)
    base_block(2)
    serve(2)
    serve(3)
    base_block(3)

    x_copies = []
    for i in range(3):
        core_copies[i].wait_recv()
        x_out[i] = (mine[i] + core_in[i]).astype(BF16)
        copy = remote(x_out.at[i], x_in.at[i], x_send.at[i], x_recv.at[i], tensor_at(2 * ORDER[i]))
        copy.start()
        x_copies.append(copy)

    pass_copies = []
    for j in range(PIECES):
        relay_copies[j].wait_recv()
        copy = remote(
            relay.at[j], a_far.at[pl.ds(DIRECT + j * PIECE, PIECE)], pass_send.at[j], pass_recv.at[j], pass_to
        )
        copy.start()
        pass_copies.append(copy)

    for o in range(1, 4):
        dst = b_near.at[o, pl.ds(0, RANK)] if o < 3 else b_far
        copy = remote(b_out.at[o - 1], dst, b_send.at[o - 1], b_recv.at[o - 1], dp_at(-o))
        copy.start()
        b_copies.append(copy)

    low_lanes = lax.broadcasted_iota(jnp.int32, (SEG, 128), 1) < RANK
    half = segs // 2

    a_copies[0].wait_recv()
    a_copies[1].wait_recv()

    def near_shrink(s):
        return nt_dot(tok[s], twice(a_near[jnp.minimum(offs[s], 2)]))

    for j in range(half):
        packed = jnp.where(low_lanes, near_shrink(j), near_shrink(j + half))
        s_mine[j] = packed
        s_out[j] = packed.astype(BF16)
    s_copies = []
    for k in range(1, n_tensor):
        copy = remote(s_out, s_in.at[k - 1], s_send.at[k - 1], s_recv.at[k - 1], tensor_at(k))
        copy.start()
        s_copies.append(copy)

    a_copies[2].wait_recv()
    for copy in pass_copies:
        copy.wait_recv()
    far = twice(a_far[...])
    first = nt_dot(tok[far_seg], far)
    second = nt_dot(tok[segs - 2], far)
    third = nt_dot(tok[segs - 1], far)
    h = SEG // 2
    packed = jnp.concatenate(
        [jnp.where(low_lanes, first, second), jnp.where(low_lanes[:h], third[:h], third[h:])], axis=0
    )
    t_mine[...] = packed
    t_out[...] = packed.astype(BF16)
    t_copies = []
    for k in range(1, n_tensor):
        copy = remote(t_out, t_in.at[k - 1], t_send.at[k - 1], t_recv.at[k - 1], tensor_at(k))
        copy.start()
        t_copies.append(copy)

    core_copies[3].wait_recv()
    for copy in x_copies:
        copy.wait_recv()
    acc[...] = (
        mine[3] + core_in[3] + x_in[0].astype(F32) + x_in[1].astype(F32) + x_in[2].astype(F32)
    )

    b_copies[0].wait_recv()
    b_copies[1].wait_recv()
    for o in (1, 2):
        b_near[o, RANK:] = b_near[o, :RANK]
    for copy in s_copies:
        copy.wait_recv()
    for j in range(half):
        total = s_mine[j]
        for k in range(n_tensor - 1):
            total = total + s_in[k, j].astype(F32)
        for s, keep in ((j, low_lanes), (j + half, ~low_lanes)):
            x = jnp.where(keep, total, 0.0).astype(BF16)
            add = jnp.dot(x, b_near[jnp.minimum(offs[s], 2)], preferred_element_type=F32)
            used = (offs[s] < 3) & (s < live_count)
            acc[s] += jnp.where(used, add, 0.0)

    b_copies[2].wait_recv()
    bf = twice(b_far[...])
    for copy in t_copies:
        copy.wait_recv()
    total = t_mine[...]
    for k in range(n_tensor - 1):
        total = total + t_in[k].astype(F32)
    top, low = total[:SEG], total[SEG:]

    def far_delta(x, keep):
        return jnp.dot(jnp.where(keep, x, 0.0).astype(BF16), bf, preferred_element_type=F32)

    first = far_delta(top, low_lanes)
    second = far_delta(top, ~low_lanes)
    third = jnp.concatenate([far_delta(low, low_lanes[:h]), far_delta(low, ~low_lanes[:h])], axis=0)
    for s in range(segs):
        add = first if s < 4 else second if s == segs - 2 else third
        used = (offs[s] == 3) & (s < live_count)
        out_ref[pl.ds(s * SEG, SEG), :] = (acc[s] + jnp.where(used, add, 0.0)).astype(out_ref.dtype)

    for copy in asks + a_copies + relay_copies + pass_copies + b_copies + core_copies + x_copies + s_copies + t_copies:
        copy.wait_send()


def per_device(n_dp, n_tensor, tokens, w, down, up, slot, ids, live):
    rows, width = tokens.shape
    segs = ids.shape[0]
    stored, rank, columns = up.shape
    peers = n_tensor - 1
    dma = pltpu.SemaphoreType.DMA
    vmem, smem = pltpu.VMEM, pltpu.SMEM
    return pl.pallas_call(
        functools.partial(kernel, n_dp, n_tensor),
        name="adapted_projection",
        out_shape=jax.ShapeDtypeStruct((rows, columns), BF16),
        in_specs=[pl.BlockSpec(memory_space=pl.ANY)] * 7,
        out_specs=pl.BlockSpec(memory_space=pltpu.VMEM),
        scratch_shapes=[
            vmem((segs, SEG, width), BF16),
            vmem((4, width, 2 * columns), BF16),
            vmem((stored, rank, width), BF16),
            vmem((stored, rank, columns), BF16),
            smem(slot.shape, jnp.int32),
            smem(ids.shape, jnp.int32),
            smem(live.shape, jnp.int32),
            vmem((3, 8, 128), jnp.int32),
            vmem((3, 8, 128), jnp.int32),
            vmem((3, rank, width), BF16),
            vmem((3, rank, width), BF16),
            vmem((rank, width), BF16),
            vmem((PIECES, PIECE, width), BF16),
            vmem((3, rank, columns), BF16),
            vmem((3, 2 * rank, columns), BF16),
            vmem((rank, columns), BF16),
            vmem((4, segs, SEG, columns), F32),
            vmem((4, segs, SEG, columns), F32),
            vmem((4, segs, SEG, columns), F32),
            vmem((3, segs, SEG, columns), BF16),
            vmem((3, segs, SEG, columns), BF16),
            vmem((segs // 2, SEG, 128), F32),
            vmem((segs // 2, SEG, 128), BF16),
            vmem((peers, segs // 2, SEG, 128), BF16),
            vmem((SEG + SEG // 2, 128), F32),
            vmem((SEG + SEG // 2, 128), BF16),
            vmem((peers, SEG + SEG // 2, 128), BF16),
            vmem((segs, SEG, columns), F32),
            dma((14,)),
            dma((3,)),
            dma((3,)),
            dma((3,)),
            dma((3,)),
            dma((PIECES,)),
            dma((PIECES,)),
            dma((PIECES,)),
            dma((PIECES,)),
            dma((3,)),
            dma((3,)),
            dma((4,)),
            dma((4,)),
            dma((3,)),
            dma((3,)),
            dma((peers,)),
            dma((peers,)),
            dma((peers,)),
            dma((peers,)),
        ],
        compiler_params=pltpu.CompilerParams(
            collective_id=0, has_side_effects=True, vmem_limit_bytes=63 * 1024 * 1024
        ),
        cost_estimate=pl.CostEstimate(flops=2_000_000_000, bytes_accessed=4_500_000, transcendentals=0),
    )(tokens.reshape(segs, SEG, width), w, down, up, slot, ids, live)


def solution(mesh):
    placed = (
        P("dp", "tensor"),
        P("tensor", None),
        P("dp", None, "tensor"),
        P("dp", None, "tensor"),
        P(),
        P("dp"),
        P("dp"),
    )
    return jax.shard_map(
        functools.partial(per_device, mesh.shape["dp"], mesh.shape["tensor"]),
        mesh=mesh,
        in_specs=placed,
        out_specs=P("dp", "tensor"),
        check_vma=False,
    )
```

```python
import functools

import jax
import jax.numpy as jnp
from jax import lax
from jax.experimental import pallas as pl
from jax.experimental.pallas import tpu as pltpu
from jax.sharding import PartitionSpec as P

MESH = pl.DeviceIdType.MESH
F32 = jnp.float32
BF16 = jnp.bfloat16

RING = 8
SEG = 128
RANK = 64
DIRECT = 16
PIECE = 16
PIECES = (RANK - DIRECT) // PIECE
STEP = 3
ORDER = (2, 1, 3, 0)


def nt_dot(a, b):
    return lax.dot_general(a, b, (((1,), (1,)), ((), ())), preferred_element_type=F32)


def twice(a):
    return jnp.concatenate([a, a], axis=0)


def kernel(
    n_dp,
    n_tensor,
    tokens_hbm,
    w_hbm,
    down_hbm,
    up_hbm,
    slot_hbm,
    ids_hbm,
    live_hbm,
    out_ref,
    tok,
    w,
    down,
    up,
    slot,
    ids,
    live,
    req_out,
    req_in,
    a_out,
    a_near,
    a_far,
    relay,
    b_out,
    b_near,
    b_far,
    mine,
    core_out,
    core_in,
    x_out,
    x_in,
    s_mine,
    s_core,
    s_out,
    s_in,
    s_all,
    t_mine,
    t_core,
    t_out,
    t_in,
    t_all,
    acc,
    load_sem,
    req_send,
    req_recv,
    a_send,
    a_recv,
    relay_send,
    relay_recv,
    pass_send,
    pass_recv,
    b_send,
    b_recv,
    core_send,
    core_recv,
    x_send,
    x_recv,
    s_send,
    s_recv,
    t_send,
    t_recv,
):
    me = lax.axis_index("dp")
    t = lax.axis_index("tensor")
    n_chip = n_tensor // 2
    segs = tok.shape[0]
    half = segs // 2
    core = lax.rem(t, 2)
    stored = down.shape[0]

    def dp_at(offset):
        return (lax.rem(me + offset + n_dp, n_dp), t)

    def tensor_at(offset):
        return (me, lax.rem(t + offset, n_tensor))

    other_core = (me, t + 1 - 2 * core)
    row = me // RING * RING
    y = lax.rem(me, RING)
    relay_to = (row + lax.rem(y + 2, RING), t)
    relay_from = (row + lax.rem(y + RING - 2, RING), t)
    pass_to = (lax.rem(row + lax.rem(y + RING - 2, RING) - 3 + n_dp, n_dp), t)
    far_owner = lax.rem(me + 3, n_dp)
    pass_from = (far_owner // RING * RING + lax.rem(lax.rem(far_owner, RING) + 2, RING), t)

    def remote(src, dst, send, recv, device):
        return pltpu.make_async_remote_copy(
            src_ref=src, dst_ref=dst, send_sem=send, recv_sem=recv, device_id=device, device_id_type=MESH
        )

    barrier = pltpu.get_barrier_semaphore()
    peers = [dp_at(o) for o in (1, 2, 3, -1, -2, -3)]
    peers += [relay_to, relay_from, pass_to, pass_from]
    peers += [tensor_at(k) for k in range(1, n_tensor)]
    for peer in peers:
        pl.semaphore_signal(barrier, inc=1, device_id=peer, device_id_type=MESH)

    small = [
        pltpu.make_async_copy(src, dst, load_sem.at[i])
        for i, (src, dst) in enumerate(((slot_hbm, slot), (ids_hbm, ids), (live_hbm, live)))
    ]
    down_load = pltpu.make_async_copy(down_hbm, down, load_sem.at[3])
    up_load = pltpu.make_async_copy(up_hbm, up, load_sem.at[4])
    tok_load = pltpu.make_async_copy(tokens_hbm, tok, load_sem.at[5])
    w_load = []
    for i, k in enumerate(ORDER):
        for side in range(2):
            owner = lax.rem(t + 2 * k, n_tensor)
            if side:
                owner = owner + 1 - 2 * lax.rem(owner, 2)
            columns = pl.ds(pl.multiple_of(owner * 128, 128), 128)
            w_load.append(
                pltpu.make_async_copy(
                    w_hbm.at[:, columns], w.at[i, :, pl.ds(side * 128, 128)], load_sem.at[6 + 2 * i + side]
                )
            )
    for copy in small:
        copy.start()
    down_load.start()
    tok_load.start()
    for copy in w_load:
        copy.start()
    up_load.start()

    for copy in small:
        copy.wait()
    offs, locs = [], []
    for s in range(segs):
        place = slot[ids[s]]
        offs.append(lax.rem(place // stored - me + n_dp, n_dp))
        locs.append(lax.rem(place, stored))
    wanted = []
    for o in range(4):
        found = jnp.int32(0)
        for s in range(4):
            found = jnp.where(offs[s] == o, locs[s], found)
        wanted.append(found)
    far_seg = jnp.int32(0)
    for s in range(4):
        far_seg = jnp.where(offs[s] == 3, s, far_seg)
    live_count = live[0]
    for o in range(1, 4):
        req_out[o - 1] = jnp.full(req_out.shape[1:], wanted[o], jnp.int32)

    pl.semaphore_wait(barrier, len(peers))
    asks = [
        remote(req_out.at[o - 1], req_in.at[o - 1], req_send.at[o - 1], req_recv.at[o - 1], dp_at(o))
        for o in range(1, 4)
    ]
    for copy in asks:
        copy.start()

    core_copies, x_copies, a_copies, relay_copies, pass_copies, b_copies = [], [], [], [], [], []

    def base_block(i):
        w_load[2 * i].wait()
        w_load[2 * i + 1].wait()
        for s in range(0, segs, STEP):
            rows = tok[pl.ds(s, STEP)].reshape(STEP * SEG, tok.shape[2])
            part = jnp.dot(rows, w[i], preferred_element_type=F32)
            mine[i, pl.ds(s * SEG, STEP * SEG), :] = part[:, :128]
            core_out[i, pl.ds(s * SEG, STEP * SEG), :] = part[:, 128:]
        copy = remote(core_out.at[i], core_in.at[i], core_send.at[i], core_recv.at[i], other_core)
        copy.start()
        core_copies.append(copy)

    def base_send(i):
        core_copies[i].wait_recv()
        x_out[i] = (mine[i] + core_in[i]).astype(BF16)
        copy = remote(x_out.at[i], x_in.at[i], x_send.at[i], x_recv.at[i], tensor_at(2 * ORDER[i]))
        copy.start()
        x_copies.append(copy)

    def serve(o):
        asks[o - 1].wait_recv()
        pick = jnp.max(req_in[o - 1])
        a_out[o - 1] = down[pick]
        b_out[o - 1] = up[pick]
        dst = a_near.at[o] if o < 3 else a_far
        rows = RANK if o < 3 else DIRECT
        if o == 3:
            for j in range(PIECES):
                copy = remote(
                    a_out.at[o - 1, pl.ds(DIRECT + j * PIECE, PIECE)],
                    relay.at[j],
                    relay_send.at[j],
                    relay_recv.at[j],
                    relay_to,
                )
                copy.start()
                relay_copies.append(copy)
        copy = remote(
            a_out.at[o - 1, pl.ds(0, rows)], dst.at[pl.ds(0, rows)], a_send.at[o - 1], a_recv.at[o - 1], dp_at(-o)
        )
        copy.start()
        a_copies.append(copy)

    tok_load.wait()
    base_block(0)
    down_load.wait()
    up_load.wait()
    a_near[0] = down[wanted[0]]
    b_near[0] = twice(up[wanted[0]])
    serve(1)
    base_block(1)
    serve(2)
    serve(3)
    base_send(0)
    base_block(2)
    base_send(1)
    base_block(3)
    base_send(2)

    for j in range(PIECES):
        relay_copies[j].wait_recv()
        copy = remote(
            relay.at[j], a_far.at[pl.ds(DIRECT + j * PIECE, PIECE)], pass_send.at[j], pass_recv.at[j], pass_to
        )
        copy.start()
        pass_copies.append(copy)

    for o in range(1, 4):
        dst = b_near.at[o, pl.ds(0, RANK)] if o < 3 else b_far
        copy = remote(b_out.at[o - 1], dst, b_send.at[o - 1], b_recv.at[o - 1], dp_at(-o))
        copy.start()
        b_copies.append(copy)

    def rows_of(part, owner):
        size = part.shape[0] // 2
        return part.at[pl.ds(pl.multiple_of(owner * size, size), size)]

    def core_phase(part, landing, sems):
        copy = remote(rows_of(part, 1 - core), landing, sems[0].at[0], sems[1].at[0], other_core)
        copy.start()
        return [copy]

    def chip_phase(part, landing, out, arrived, sems, copies):
        copies[0].wait_recv()
        landing[...] = rows_of(part, core)[...] + landing[...]
        out[...] = landing[...].astype(BF16)
        for k in range(1, n_chip):
            copy = remote(out, arrived.at[k - 1], sems[0].at[k], sems[1].at[k], tensor_at(2 * k))
            copy.start()
            copies.append(copy)

    def swap_phase(landing, arrived, total, sems, copies):
        for k in range(1, n_chip):
            copies[k].wait_recv()
        rows = landing[...]
        for k in range(1, n_chip):
            rows = rows + arrived[k - 1].astype(F32)
        rows_of(total, core)[...] = rows.astype(BF16)
        copy = remote(
            rows_of(total, core), rows_of(total, core), sems[0].at[n_chip], sems[1].at[n_chip], other_core
        )
        copy.start()
        copies.append(copy)

    low_lanes = lax.broadcasted_iota(jnp.int32, (SEG, 128), 1) < RANK

    def seg_rows(s):
        return pl.ds(s * SEG, SEG)

    a_copies[0].wait_recv()
    a_copies[1].wait_recv()

    def near_shrink(s):
        return nt_dot(tok[s], twice(a_near[jnp.minimum(offs[s], 2)]))

    for j in range(half):
        s_mine[seg_rows(j), :] = jnp.where(low_lanes, near_shrink(j), near_shrink(j + half))
    s_sems, t_sems = (s_send, s_recv), (t_send, t_recv)
    s_copies = core_phase(s_mine, s_core, s_sems)
    chip_phase(s_mine, s_core, s_out, s_in, s_sems, s_copies)

    a_copies[2].wait_recv()
    for copy in pass_copies:
        copy.wait_recv()
    far = twice(a_far[...])
    first = nt_dot(tok[far_seg], far)
    second = nt_dot(tok[segs - 2], far)
    third = nt_dot(tok[segs - 1], far)
    h = SEG // 2
    t_mine[pl.ds(0, SEG), :] = jnp.where(low_lanes, first, second)
    t_mine[pl.ds(SEG, h), :] = jnp.where(low_lanes[:h], third[:h], third[h:])
    t_copies = core_phase(t_mine, t_core, t_sems)

    core_copies[3].wait_recv()
    for copy in x_copies:
        copy.wait_recv()
    acc[...] = mine[3] + core_in[3] + x_in[0].astype(F32) + x_in[1].astype(F32) + x_in[2].astype(F32)

    chip_phase(t_mine, t_core, t_out, t_in, t_sems, t_copies)
    swap_phase(s_core, s_in, s_all, s_sems, s_copies)

    b_copies[0].wait_recv()
    b_copies[1].wait_recv()
    for o in (1, 2):
        b_near[o, RANK:] = b_near[o, :RANK]
    s_copies[-1].wait_recv()
    for j in range(half):
        total = s_all[seg_rows(j), :]
        for s, keep in ((j, low_lanes), (j + half, ~low_lanes)):
            x = jnp.where(keep, total, jnp.zeros_like(total))
            add = jnp.dot(x, b_near[jnp.minimum(offs[s], 2)], preferred_element_type=F32)
            used = (offs[s] < 3) & (s < live_count)
            acc[seg_rows(s), :] += jnp.where(used, add, 0.0)

    b_copies[2].wait_recv()
    bf = twice(b_far[...])
    swap_phase(t_core, t_in, t_all, t_sems, t_copies)
    t_copies[-1].wait_recv()
    top, low = t_all[pl.ds(0, SEG), :], t_all[pl.ds(SEG, h), :]

    def far_delta(x, keep):
        return jnp.dot(jnp.where(keep, x, jnp.zeros_like(x)), bf, preferred_element_type=F32)

    first = far_delta(top, low_lanes)
    second = far_delta(top, ~low_lanes)
    third = jnp.concatenate([far_delta(low, low_lanes[:h]), far_delta(low, ~low_lanes[:h])], axis=0)
    for s in range(segs):
        add = first if s < 4 else second if s == segs - 2 else third
        used = (offs[s] == 3) & (s < live_count)
        out_ref[seg_rows(s), :] = (acc[seg_rows(s), :] + jnp.where(used, add, 0.0)).astype(out_ref.dtype)

    for copy in asks + a_copies + relay_copies + pass_copies + b_copies + core_copies + x_copies + s_copies + t_copies:
        copy.wait_send()


def per_device(n_dp, n_tensor, tokens, w, down, up, slot, ids, live):
    rows, width = tokens.shape
    segs = ids.shape[0]
    stored, rank, columns = up.shape
    chips = n_tensor // 2
    near, far = rows // 2, SEG + SEG // 2
    dma = pltpu.SemaphoreType.DMA
    vmem, smem = pltpu.VMEM, pltpu.SMEM
    return pl.pallas_call(
        functools.partial(kernel, n_dp, n_tensor),
        name="adapted_projection",
        out_shape=pltpu.VMEM((rows, columns), BF16),
        in_specs=[pl.BlockSpec(memory_space=pl.ANY)] * 7,
        out_specs=pl.BlockSpec(memory_space=pltpu.VMEM),
        scratch_shapes=[
            vmem((segs, SEG, width), BF16),
            vmem((4, width, 2 * columns), BF16),
            vmem((stored, rank, width), BF16),
            vmem((stored, rank, columns), BF16),
            smem(slot.shape, jnp.int32),
            smem(ids.shape, jnp.int32),
            smem(live.shape, jnp.int32),
            vmem((3, 8, 128), jnp.int32),
            vmem((3, 8, 128), jnp.int32),
            vmem((3, rank, width), BF16),
            vmem((3, rank, width), BF16),
            vmem((rank, width), BF16),
            vmem((PIECES, PIECE, width), BF16),
            vmem((3, rank, columns), BF16),
            vmem((3, 2 * rank, columns), BF16),
            vmem((rank, columns), BF16),
            vmem((4, rows, columns), F32),
            vmem((4, rows, columns), F32),
            vmem((4, rows, columns), F32),
            vmem((3, rows, columns), BF16),
            vmem((3, rows, columns), BF16),
            vmem((near, 128), F32),
            vmem((near // 2, 128), F32),
            vmem((near // 2, 128), BF16),
            vmem((chips - 1, near // 2, 128), BF16),
            vmem((near, 128), BF16),
            vmem((far, 128), F32),
            vmem((far // 2, 128), F32),
            vmem((far // 2, 128), BF16),
            vmem((chips - 1, far // 2, 128), BF16),
            vmem((far, 128), BF16),
            vmem((rows, columns), F32),
            dma((14,)),
            dma((3,)),
            dma((3,)),
            dma((3,)),
            dma((3,)),
            dma((PIECES,)),
            dma((PIECES,)),
            dma((PIECES,)),
            dma((PIECES,)),
            dma((3,)),
            dma((3,)),
            dma((4,)),
            dma((4,)),
            dma((3,)),
            dma((3,)),
            dma((chips + 1,)),
            dma((chips + 1,)),
            dma((chips + 1,)),
            dma((chips + 1,)),
        ],
        compiler_params=pltpu.CompilerParams(
            collective_id=0, has_side_effects=True, vmem_limit_bytes=63 * 1024 * 1024
        ),
        cost_estimate=pl.CostEstimate(flops=2_000_000_000, bytes_accessed=4_500_000, transcendentals=0),
    )(tokens.reshape(segs, SEG, width), w, down, up, slot, ids, live)


def solution(mesh):
    placed = (
        P("dp", "tensor"),
        P("tensor", None),
        P("dp", None, "tensor"),
        P("dp", None, "tensor"),
        P(),
        P("dp"),
        P("dp"),
    )
    return jax.shard_map(
        functools.partial(per_device, mesh.shape["dp"], mesh.shape["tensor"]),
        mesh=mesh,
        in_specs=placed,
        out_specs=P("dp", "tensor"),
        check_vma=False,
    )
```

```python
import functools

import jax
import jax.numpy as jnp
from jax import lax
from jax.experimental import pallas as pl
from jax.experimental.pallas import tpu as pltpu
from jax.sharding import PartitionSpec as P

MESH = pl.DeviceIdType.MESH
F32 = jnp.float32
BF16 = jnp.bfloat16

RING = 8
SEG = 128
RANK = 64
HALF = RANK // 2
SHORT = 384
PIECES = ((384, 256), (640, 384))
GROUPS = 128 // HALF
STEP = 3
ORDER = (2, 1, 3, 0)


def nt_dot(a, b):
    return lax.dot_general(a, b, (((1,), (1,)), ((), ())), preferred_element_type=F32)


def kernel(
    n_dp,
    n_tensor,
    tokens_hbm,
    w_hbm,
    down_hbm,
    up_hbm,
    slot_hbm,
    ids_hbm,
    live_hbm,
    out_ref,
    tok,
    tok_other,
    w,
    down,
    up,
    slot,
    ids,
    live,
    req_out,
    req_in,
    a_out,
    a_in,
    relay,
    b_out,
    b_in,
    b_relay,
    mine,
    core_out,
    core_in,
    x_out,
    x_in,
    s_mine,
    s_out,
    s_in,
    s_all,
    acc,
    load_sem,
    req_send,
    req_recv,
    a_send,
    a_recv,
    swap_send,
    swap_recv,
    relay_send,
    relay_recv,
    pass_send,
    pass_recv,
    b_send,
    b_recv,
    core_send,
    core_recv,
    x_send,
    x_recv,
    s_send,
    s_recv,
):
    me = lax.axis_index("dp")
    t = lax.axis_index("tensor")
    n_chip = n_tensor // 2
    segs = tok.shape[0]
    stored = down.shape[0]

    core = lax.rem(t, 2)
    sides = (t, t + 1 - 2 * core)

    def dp_at(offset, cross=0):
        return (lax.rem(me + offset + n_dp, n_dp), sides[cross])

    def tensor_at(offset):
        return (me, lax.rem(t + offset, n_tensor))

    other_core = (me, sides[1])
    row = me // RING * RING
    y = lax.rem(me, RING)
    relay_to = (row + lax.rem(y + 2, RING), t)
    relay_from = (row + lax.rem(y + RING - 2, RING), t)
    pass_index = lax.rem(row + lax.rem(y + RING - 2, RING) - 3 + n_dp, n_dp)
    pass_to = [(pass_index, side) for side in sides]
    far_owner = lax.rem(me + 3, n_dp)
    from_index = far_owner // RING * RING + lax.rem(lax.rem(far_owner, RING) + 2, RING)
    pass_from = [(from_index, side) for side in sides]

    def remote(src, dst, send, recv, device):
        return pltpu.make_async_remote_copy(
            src_ref=src, dst_ref=dst, send_sem=send, recv_sem=recv, device_id=device, device_id_type=MESH
        )

    barrier = pltpu.get_barrier_semaphore()
    peers = [dp_at(o, cross) for o in (1, 2, 3, -1, -2, -3) for cross in range(2)]
    peers += [relay_to, relay_from, *pass_to, *pass_from]
    peers += [tensor_at(k) for k in range(1, n_tensor)]
    for peer in peers:
        pl.semaphore_signal(barrier, inc=1, device_id=peer, device_id_type=MESH)

    small = [
        pltpu.make_async_copy(src, dst, load_sem.at[i])
        for i, (src, dst) in enumerate(((slot_hbm, slot), (ids_hbm, ids), (live_hbm, live)))
    ]
    down_load = pltpu.make_async_copy(down_hbm, down, load_sem.at[3])
    up_load = pltpu.make_async_copy(up_hbm, up, load_sem.at[4])
    tok_load = pltpu.make_async_copy(tokens_hbm, tok, load_sem.at[5])
    w_load = []
    for i, k in enumerate(ORDER):
        for side in range(2):
            owner = lax.rem(t + 2 * k, n_tensor)
            if side:
                owner = owner + 1 - 2 * lax.rem(owner, 2)
            columns = pl.ds(pl.multiple_of(owner * 128, 128), 128)
            w_load.append(
                pltpu.make_async_copy(
                    w_hbm.at[:, columns], w.at[i, :, pl.ds(side * 128, 128)], load_sem.at[6 + 2 * i + side]
                )
            )
    for copy in small:
        copy.start()
    down_load.start()
    tok_load.start()
    for copy in w_load:
        copy.start()
    up_load.start()

    for copy in small:
        copy.wait()
    offs, locs = [], []
    for s in range(segs):
        place = slot[ids[s]]
        offs.append(lax.rem(place // stored - me + n_dp, n_dp))
        locs.append(lax.rem(place, stored))
    wanted = []
    for o in range(4):
        found = jnp.int32(0)
        for s in range(4):
            found = jnp.where(offs[s] == o, locs[s], found)
        wanted.append(found)
    far_seg = jnp.int32(0)
    for s in range(4):
        far_seg = jnp.where(offs[s] == 3, s, far_seg)
    live_count = live[0]
    for o in range(1, 4):
        req_out[o - 1] = jnp.full(req_out.shape[1:], wanted[o], jnp.int32)

    pl.semaphore_wait(barrier, len(peers))
    asks = [
        remote(req_out.at[o - 1], req_in.at[o - 1], req_send.at[o - 1], req_recv.at[o - 1], dp_at(o))
        for o in range(1, 4)
    ]
    for copy in asks:
        copy.start()

    core_copies, x_copies, a_copies, swap_copies, relay_copies, pass_copies, b_copies = [], [], [], [], [], [], []

    def base_block(i):
        w_load[2 * i].wait()
        w_load[2 * i + 1].wait()
        for s in range(0, segs, STEP):
            rows = tok[pl.ds(s, STEP)].reshape(STEP * SEG, tok.shape[2])
            part = jnp.dot(rows, w[i], preferred_element_type=F32)
            mine[i, pl.ds(s * SEG, STEP * SEG), :] = part[:, :128]
            core_out[i, pl.ds(s * SEG, STEP * SEG), :] = part[:, 128:]
        copy = remote(core_out.at[i], core_in.at[i], core_send.at[i], core_recv.at[i], other_core)
        copy.start()
        core_copies.append(copy)

    def base_send(i):
        core_copies[i].wait_recv()
        x_out[i] = (mine[i] + core_in[i]).astype(BF16)
        copy = remote(x_out.at[i], x_in.at[i], x_send.at[i], x_recv.at[i], tensor_at(2 * ORDER[i]))
        copy.start()
        x_copies.append(copy)

    def start(copies, *what):
        copy = remote(*what)
        copy.start()
        copies.append(copy)

    def rank_half(cross):
        start_row = (1 - core) * HALF if cross else core * HALF
        return pl.ds(pl.multiple_of(start_row, HALF), HALF)

    def serve(o, crosses=(0, 1), again=False):
        if not again:
            asks[o - 1].wait_recv()
            pick = jnp.max(req_in[o - 1])
            a_out[o] = down[pick]
            b_out[o - 1] = up[pick]
        if o == 3:
            for p, (first, size) in enumerate(PIECES):
                for cross in range(2):
                    n = 2 * p + cross
                    src = a_out.at[o, rank_half(cross), pl.ds(first, size)]
                    start(relay_copies, src, relay.at[cross, :, pl.ds(first - SHORT, size)], relay_send.at[n], relay_recv.at[n], relay_to)
        for cross in crosses:
            lanes = pl.ds(0, a_out.shape[2] if o < 3 else SHORT)
            src = a_out.at[o, rank_half(cross), lanes]
            n = 2 * (o - 1) + cross
            start(a_copies, src, a_in.at[o, cross, :, lanes], a_send.at[n], a_recv.at[n], dp_at(-o, cross))

    def pass_on(p, cross):
        n = 2 * p + cross
        relay_copies[n].wait_recv()
        first, size = PIECES[p]
        src = relay.at[cross, :, pl.ds(first - SHORT, size)]
        dst = a_in.at[3, cross, :, pl.ds(first, size)]
        start(pass_copies, src, dst, pass_send.at[n], pass_recv.at[n], pass_to[cross])

    tok_load.wait()
    base_block(0)
    down_load.wait()
    up_load.wait()
    a_out[0] = down[wanted[0]]
    a_in[0, 0] = a_out[0, rank_half(0)]
    b_in[0] = up[wanted[0]]
    serve(1, (0,))
    base_block(1)
    serve(2, (0,))
    serve(3)
    serve(2, (1,), True)
    serve(1, (1,), True)
    base_send(0)
    base_block(2)
    base_send(1)
    base_block(3)
    base_send(2)
    start(swap_copies, tok, tok_other, swap_send.at[0], swap_recv.at[0], other_core)
    start(swap_copies, a_out.at[0, rank_half(1)], a_in.at[0, 1], swap_send.at[1], swap_recv.at[1], other_core)
    for p in range(len(PIECES)):
        for cross in range(2):
            pass_on(p, cross)
    n = 2 * len(PIECES)
    start(relay_copies, b_out.at[2], b_relay, relay_send.at[n], relay_recv.at[n], relay_to)

    lane_group = lax.broadcasted_iota(jnp.int32, (SEG, 128), 1) // HALF
    row_group = lax.broadcasted_iota(jnp.int32, (SEG, 128), 0) // HALF
    own_group = lane_group == row_group

    def spread(a):
        return jnp.concatenate([a] * GROUPS, axis=0)

    for copy in swap_copies + a_copies + pass_copies:
        copy.wait_recv()
    for s in range(segs):
        o = jnp.minimum(offs[s], 3)
        part = nt_dot(tok[s], spread(a_in[o, 0])) + nt_dot(tok_other[s], spread(a_in[o, 1]))
        kept = jnp.where(own_group, part, 0.0)
        packed = kept[:HALF]
        for g in range(1, GROUPS):
            packed = packed + kept[g * HALF : (g + 1) * HALF]
        s_mine[s] = packed
        s_out[s] = packed.astype(BF16)
    s_copies = []
    for k in range(1, n_chip):
        start(s_copies, s_out, s_in.at[k - 1], s_send.at[k - 1], s_recv.at[k - 1], tensor_at(2 * k))

    for o in (1, 2):
        start(b_copies, b_out.at[o - 1], b_in.at[o], b_send.at[o - 1], b_recv.at[o - 1], dp_at(-o))
    relay_copies[n].wait_recv()
    start(b_copies, b_relay, b_in.at[3], b_send.at[2], b_recv.at[2], pass_to[0])

    core_copies[3].wait_recv()
    for copy in x_copies:
        copy.wait_recv()
    acc[...] = mine[3] + core_in[3] + x_in[0].astype(F32) + x_in[1].astype(F32) + x_in[2].astype(F32)

    for copy in s_copies:
        copy.wait_recv()
    total = s_mine[...]
    for k in range(n_chip - 1):
        total = total + s_in[k].astype(F32)
    s_all[core] = total.astype(BF16)
    start(s_copies, s_all.at[core], s_all.at[core], s_send.at[n_chip - 1], s_recv.at[n_chip - 1], other_core)

    for copy in b_copies:
        copy.wait_recv()
    s_copies[-1].wait_recv()
    for s in range(segs):
        factor = b_in[jnp.minimum(offs[s], 3)]
        add = None
        for h in range(2):
            x = jnp.where(own_group, spread(s_all[h, s].astype(F32)), 0.0).astype(BF16)
            term = jnp.dot(x, spread(factor[h * HALF : (h + 1) * HALF]), preferred_element_type=F32)
            add = term if add is None else add + term
        add = jnp.where(s < live_count, add, 0.0)
        rows = pl.ds(s * SEG, SEG)
        out_ref[rows, :] = (acc[rows, :] + add).astype(out_ref.dtype)

    for copy in asks + a_copies + swap_copies + relay_copies + pass_copies + b_copies + core_copies + x_copies + s_copies:
        copy.wait_send()


def per_device(n_dp, n_tensor, tokens, w, down, up, slot, ids, live):
    rows, width = tokens.shape
    segs = ids.shape[0]
    stored, rank, columns = up.shape
    chips = n_tensor // 2
    dma = pltpu.SemaphoreType.DMA
    vmem, smem = pltpu.VMEM, pltpu.SMEM
    return pl.pallas_call(
        functools.partial(kernel, n_dp, n_tensor),
        name="adapted_projection",
        out_shape=pltpu.VMEM((rows, columns), BF16),
        in_specs=[pl.BlockSpec(memory_space=pl.ANY)] * 7,
        out_specs=pl.BlockSpec(memory_space=pltpu.VMEM),
        scratch_shapes=[
            vmem((segs, SEG, width), BF16),
            vmem((segs, SEG, width), BF16),
            vmem((4, width, 2 * columns), BF16),
            vmem((stored, rank, width), BF16),
            vmem((stored, rank, columns), BF16),
            smem(slot.shape, jnp.int32),
            smem(ids.shape, jnp.int32),
            smem(live.shape, jnp.int32),
            vmem((3, 8, 128), jnp.int32),
            vmem((3, 8, 128), jnp.int32),
            vmem((4, rank, width), BF16),
            vmem((4, 2, HALF, width), BF16),
            vmem((2, HALF, width - SHORT), BF16),
            vmem((3, rank, columns), BF16),
            vmem((4, rank, columns), BF16),
            vmem((rank, columns), BF16),
            vmem((4, rows, columns), F32),
            vmem((4, rows, columns), F32),
            vmem((4, rows, columns), F32),
            vmem((3, rows, columns), BF16),
            vmem((3, rows, columns), BF16),
            vmem((segs, HALF, 128), F32),
            vmem((segs, HALF, 128), BF16),
            vmem((chips - 1, segs, HALF, 128), BF16),
            vmem((2, segs, HALF, 128), BF16),
            vmem((rows, columns), F32),
            dma((14,)),
            dma((3,)),
            dma((3,)),
            dma((6,)),
            dma((6,)),
            dma((2,)),
            dma((2,)),
            dma((2 * len(PIECES) + 1,)),
            dma((2 * len(PIECES) + 1,)),
            dma((2 * len(PIECES),)),
            dma((2 * len(PIECES),)),
            dma((3,)),
            dma((3,)),
            dma((4,)),
            dma((4,)),
            dma((3,)),
            dma((3,)),
            dma((chips,)),
            dma((chips,)),
        ],
        compiler_params=pltpu.CompilerParams(
            collective_id=0, has_side_effects=True, vmem_limit_bytes=63 * 1024 * 1024
        ),
        cost_estimate=pl.CostEstimate(flops=2_000_000_000, bytes_accessed=4_500_000, transcendentals=0),
    )(tokens.reshape(segs, SEG, width), w, down, up, slot, ids, live)


def solution(mesh):
    placed = (
        P("dp", "tensor"),
        P("tensor", None),
        P("dp", None, "tensor"),
        P("dp", None, "tensor"),
        P(),
        P("dp"),
        P("dp"),
    )
    return jax.shard_map(
        functools.partial(per_device, mesh.shape["dp"], mesh.shape["tensor"]),
        mesh=mesh,
        in_specs=placed,
        out_specs=P("dp", "tensor"),
        check_vma=False,
    )
```

```python
import functools

import jax
import jax.numpy as jnp
from jax import lax
from jax.experimental import pallas as pl
from jax.experimental.pallas import tpu as pltpu
from jax.sharding import PartitionSpec as P

MESH = pl.DeviceIdType.MESH
F32 = jnp.float32
BF16 = jnp.bfloat16

RING = 8
SEG = 128
RANK = 64
HALF = RANK // 2
SHORT = 384
PIECES = ((384, 256), (640, 384))
GROUPS = 128 // HALF
STEP = 3
ORDER = (2, 1, 3, 0)


def nt_dot(a, b):
    return lax.dot_general(a, b, (((1,), (1,)), ((), ())), preferred_element_type=F32)


def kernel(
    n_dp,
    n_tensor,
    tokens_hbm,
    w_hbm,
    down_hbm,
    up_hbm,
    slot_hbm,
    ids_hbm,
    live_hbm,
    out_ref,
    tok,
    tok_other,
    w,
    down,
    up,
    slot,
    ids,
    live,
    req_out,
    req_in,
    a_out,
    a_in,
    relay,
    b_out,
    b_in,
    b_relay,
    mine,
    core_out,
    core_in,
    x_out,
    x_in,
    s_mine,
    s_out,
    s_in,
    s_all,
    acc,
    load_sem,
    req_send,
    req_recv,
    a_send,
    a_recv,
    swap_send,
    swap_recv,
    relay_send,
    relay_recv,
    pass_send,
    pass_recv,
    b_send,
    b_recv,
    core_send,
    core_recv,
    x_send,
    x_recv,
    s_send,
    s_recv,
):
    me = lax.axis_index("dp")
    t = lax.axis_index("tensor")
    n_chip = n_tensor // 2
    segs = tok.shape[0]
    stored = down.shape[0]

    core = lax.rem(t, 2)
    sides = (t, t + 1 - 2 * core)

    def dp_at(offset, cross=0):
        return (lax.rem(me + offset + n_dp, n_dp), sides[cross])

    def tensor_at(offset):
        return (me, lax.rem(t + offset, n_tensor))

    other_core = (me, sides[1])
    row = me // RING * RING
    y = lax.rem(me, RING)
    relay_to = (row + lax.rem(y + 2, RING), t)
    relay_from = (row + lax.rem(y + RING - 2, RING), t)
    pass_index = lax.rem(row + lax.rem(y + RING - 2, RING) - 3 + n_dp, n_dp)
    pass_to = [(pass_index, side) for side in sides]

    def remote(src, dst, send, recv, device):
        return pltpu.make_async_remote_copy(
            src_ref=src, dst_ref=dst, send_sem=send, recv_sem=recv, device_id=device, device_id_type=MESH
        )

    barrier = pltpu.get_barrier_semaphore()
    peers = [dp_at(o) for o in (-1, -2, -3)] + [relay_from]
    peers += [tensor_at(k) for k in range(1, n_tensor)]
    for peer in peers:
        pl.semaphore_signal(barrier, inc=1, device_id=peer, device_id_type=MESH)

    small = [
        pltpu.make_async_copy(src, dst, load_sem.at[i])
        for i, (src, dst) in enumerate(((slot_hbm, slot), (ids_hbm, ids), (live_hbm, live)))
    ]
    down_load = pltpu.make_async_copy(down_hbm, down, load_sem.at[3])
    up_load = pltpu.make_async_copy(up_hbm, up, load_sem.at[4])
    tok_load = pltpu.make_async_copy(tokens_hbm, tok, load_sem.at[5])
    w_load = []
    for i, k in enumerate(ORDER):
        for side in range(2):
            owner = lax.rem(t + 2 * k, n_tensor)
            if side:
                owner = owner + 1 - 2 * lax.rem(owner, 2)
            columns = pl.ds(pl.multiple_of(owner * 128, 128), 128)
            w_load.append(
                pltpu.make_async_copy(
                    w_hbm.at[:, columns], w.at[i, :, pl.ds(side * 128, 128)], load_sem.at[6 + 2 * i + side]
                )
            )
    for copy in small:
        copy.start()
    down_load.start()
    tok_load.start()
    for copy in w_load:
        copy.start()
    up_load.start()

    for copy in small:
        copy.wait()
    offs, locs = [], []
    for s in range(segs):
        place = slot[ids[s]]
        offs.append(lax.rem(place // stored - me + n_dp, n_dp))
        locs.append(lax.rem(place, stored))
    wanted = []
    for o in range(4):
        found = jnp.int32(0)
        for s in range(4):
            found = jnp.where(offs[s] == o, locs[s], found)
        wanted.append(found)
    far_seg = jnp.int32(0)
    for s in range(4):
        far_seg = jnp.where(offs[s] == 3, s, far_seg)
    live_count = live[0]
    for o in range(1, 4):
        req_out[o - 1] = jnp.full(req_out.shape[1:], wanted[o], jnp.int32)

    pl.semaphore_wait(barrier, len(peers))
    asks = [
        remote(req_out.at[o - 1], req_in.at[o - 1], req_send.at[o - 1], req_recv.at[o - 1], dp_at(o))
        for o in range(1, 4)
    ]
    for copy in asks:
        copy.start()

    core_copies, x_copies, a_copies, swap_copies, relay_copies, pass_copies, b_copies = [], [], [], [], [], [], []

    def base_block(i):
        w_load[2 * i].wait()
        w_load[2 * i + 1].wait()
        for s in range(0, segs, STEP):
            rows = tok[pl.ds(s, STEP)].reshape(STEP * SEG, tok.shape[2])
            part = jnp.dot(rows, w[i], preferred_element_type=F32)
            mine[i, pl.ds(s * SEG, STEP * SEG), :] = part[:, :128]
            core_out[i, pl.ds(s * SEG, STEP * SEG), :] = part[:, 128:]
        copy = remote(core_out.at[i], core_in.at[i], core_send.at[i], core_recv.at[i], other_core)
        copy.start()
        core_copies.append(copy)

    def base_send(i):
        core_copies[i].wait_recv()
        x_out[i] = (mine[i] + core_in[i]).astype(BF16)
        copy = remote(x_out.at[i], x_in.at[i], x_send.at[i], x_recv.at[i], tensor_at(2 * ORDER[i]))
        copy.start()
        x_copies.append(copy)

    def start(copies, *what):
        copy = remote(*what)
        copy.start()
        copies.append(copy)

    def rank_half(cross):
        start_row = (1 - core) * HALF if cross else core * HALF
        return pl.ds(pl.multiple_of(start_row, HALF), HALF)

    def serve(o, crosses=(0, 1), again=False):
        if not again:
            asks[o - 1].wait_recv()
            pick = jnp.max(req_in[o - 1])
            a_out[o] = down[pick]
            b_out[o - 1] = up[pick]
        if o == 3:
            for p, (first, size) in enumerate(PIECES):
                for cross in range(2):
                    n = 2 * p + cross
                    src = a_out.at[o, rank_half(cross), pl.ds(first, size)]
                    start(relay_copies, src, relay.at[cross, :, pl.ds(first - SHORT, size)], relay_send.at[n], relay_recv.at[n], relay_to)
        for cross in crosses:
            lanes = pl.ds(0, a_out.shape[2] if o < 3 else SHORT)
            src = a_out.at[o, rank_half(cross), lanes]
            n = 2 * (o - 1) + cross
            start(a_copies, src, a_in.at[o, cross, :, lanes], a_send.at[n], a_recv.at[n], dp_at(-o, cross))

    def pass_on(p, cross):
        n = 2 * p + cross
        relay_copies[n].wait_recv()
        first, size = PIECES[p]
        src = relay.at[cross, :, pl.ds(first - SHORT, size)]
        dst = a_in.at[3, cross, :, pl.ds(first, size)]
        start(pass_copies, src, dst, pass_send.at[n], pass_recv.at[n], pass_to[cross])

    tok_load.wait()
    base_block(0)
    base_block(1)
    down_load.wait()
    up_load.wait()
    a_out[0] = down[wanted[0]]
    a_in[0, 0] = a_out[0, rank_half(0)]
    b_in[0] = up[wanted[0]]
    base_block(2)
    base_block(3)
    base_send(0)
    serve(1, (0,))
    serve(2, (0,))
    serve(3)
    serve(2, (1,), True)
    serve(1, (1,), True)
    base_send(1)
    base_send(2)
    start(swap_copies, tok, tok_other, swap_send.at[0], swap_recv.at[0], other_core)
    start(swap_copies, a_out.at[0, rank_half(1)], a_in.at[0, 1], swap_send.at[1], swap_recv.at[1], other_core)
    for p in range(len(PIECES)):
        for cross in range(2):
            pass_on(p, cross)
    n = 2 * len(PIECES)
    start(relay_copies, b_out.at[2], b_relay, relay_send.at[n], relay_recv.at[n], relay_to)

    lane_group = lax.broadcasted_iota(jnp.int32, (SEG, 128), 1) // HALF
    row_group = lax.broadcasted_iota(jnp.int32, (SEG, 128), 0) // HALF
    own_group = lane_group == row_group

    def spread(a):
        return jnp.concatenate([a] * GROUPS, axis=0)

    for copy in swap_copies + a_copies + pass_copies:
        copy.wait_recv()
    for s in range(segs):
        o = jnp.minimum(offs[s], 3)
        part = nt_dot(tok[s], spread(a_in[o, 0])) + nt_dot(tok_other[s], spread(a_in[o, 1]))
        kept = jnp.where(own_group, part, 0.0)
        packed = kept[:HALF]
        for g in range(1, GROUPS):
            packed = packed + kept[g * HALF : (g + 1) * HALF]
        s_mine[s] = packed
        s_out[s] = packed.astype(BF16)
    s_copies = []
    for k in range(1, n_chip):
        start(s_copies, s_out, s_in.at[k - 1], s_send.at[k - 1], s_recv.at[k - 1], tensor_at(2 * k))

    for o in (1, 2):
        start(b_copies, b_out.at[o - 1], b_in.at[o], b_send.at[o - 1], b_recv.at[o - 1], dp_at(-o))
    relay_copies[n].wait_recv()
    start(b_copies, b_relay, b_in.at[3], b_send.at[2], b_recv.at[2], pass_to[0])

    core_copies[3].wait_recv()
    for copy in x_copies:
        copy.wait_recv()
    acc[...] = mine[3] + core_in[3] + x_in[0].astype(F32) + x_in[1].astype(F32) + x_in[2].astype(F32)

    for copy in s_copies:
        copy.wait_recv()
    total = s_mine[...]
    for k in range(n_chip - 1):
        total = total + s_in[k].astype(F32)
    s_all[core] = total.astype(BF16)
    start(s_copies, s_all.at[core], s_all.at[core], s_send.at[n_chip - 1], s_recv.at[n_chip - 1], other_core)

    for copy in b_copies:
        copy.wait_recv()
    s_copies[-1].wait_recv()
    for s in range(segs):
        factor = b_in[jnp.minimum(offs[s], 3)]
        add = None
        for h in range(2):
            x = jnp.where(own_group, spread(s_all[h, s].astype(F32)), 0.0).astype(BF16)
            term = jnp.dot(x, spread(factor[h * HALF : (h + 1) * HALF]), preferred_element_type=F32)
            add = term if add is None else add + term
        add = jnp.where(s < live_count, add, 0.0)
        rows = pl.ds(s * SEG, SEG)
        out_ref[rows, :] = (acc[rows, :] + add).astype(out_ref.dtype)

    for copy in asks + a_copies + swap_copies + relay_copies + pass_copies + b_copies + core_copies + x_copies + s_copies:
        copy.wait_send()


def per_device(n_dp, n_tensor, tokens, w, down, up, slot, ids, live):
    rows, width = tokens.shape
    segs = ids.shape[0]
    stored, rank, columns = up.shape
    chips = n_tensor // 2
    dma = pltpu.SemaphoreType.DMA
    vmem, smem = pltpu.VMEM, pltpu.SMEM
    return pl.pallas_call(
        functools.partial(kernel, n_dp, n_tensor),
        name="adapted_projection",
        out_shape=pltpu.VMEM((rows, columns), BF16),
        in_specs=[pl.BlockSpec(memory_space=pl.ANY)] * 7,
        out_specs=pl.BlockSpec(memory_space=pltpu.VMEM),
        scratch_shapes=[
            vmem((segs, SEG, width), BF16),
            vmem((segs, SEG, width), BF16),
            vmem((4, width, 2 * columns), BF16),
            vmem((stored, rank, width), BF16),
            vmem((stored, rank, columns), BF16),
            smem(slot.shape, jnp.int32),
            smem(ids.shape, jnp.int32),
            smem(live.shape, jnp.int32),
            vmem((3, 8, 128), jnp.int32),
            vmem((3, 8, 128), jnp.int32),
            vmem((4, rank, width), BF16),
            vmem((4, 2, HALF, width), BF16),
            vmem((2, HALF, width - SHORT), BF16),
            vmem((3, rank, columns), BF16),
            vmem((4, rank, columns), BF16),
            vmem((rank, columns), BF16),
            vmem((4, rows, columns), F32),
            vmem((4, rows, columns), F32),
            vmem((4, rows, columns), F32),
            vmem((3, rows, columns), BF16),
            vmem((3, rows, columns), BF16),
            vmem((segs, HALF, 128), F32),
            vmem((segs, HALF, 128), BF16),
            vmem((chips - 1, segs, HALF, 128), BF16),
            vmem((2, segs, HALF, 128), BF16),
            vmem((rows, columns), F32),
            dma((14,)),
            dma((3,)),
            dma((3,)),
            dma((6,)),
            dma((6,)),
            dma((2,)),
            dma((2,)),
            dma((2 * len(PIECES) + 1,)),
            dma((2 * len(PIECES) + 1,)),
            dma((2 * len(PIECES),)),
            dma((2 * len(PIECES),)),
            dma((3,)),
            dma((3,)),
            dma((4,)),
            dma((4,)),
            dma((3,)),
            dma((3,)),
            dma((chips,)),
            dma((chips,)),
        ],
        compiler_params=pltpu.CompilerParams(
            collective_id=0, has_side_effects=True, vmem_limit_bytes=63 * 1024 * 1024
        ),
        cost_estimate=pl.CostEstimate(flops=2_000_000_000, bytes_accessed=4_500_000, transcendentals=0),
    )(tokens.reshape(segs, SEG, width), w, down, up, slot, ids, live)


def solution(mesh):
    placed = (
        P("dp", "tensor"),
        P("tensor", None),
        P("dp", None, "tensor"),
        P("dp", None, "tensor"),
        P(),
        P("dp"),
        P("dp"),
    )
    return jax.shard_map(
        functools.partial(per_device, mesh.shape["dp"], mesh.shape["tensor"]),
        mesh=mesh,
        in_specs=placed,
        out_specs=P("dp", "tensor"),
        check_vma=False,
    )
```

```python
import functools

import jax
import jax.numpy as jnp
from jax import lax
from jax.experimental import pallas as pl
from jax.experimental.pallas import tpu as pltpu
from jax.sharding import PartitionSpec as P

MESH = pl.DeviceIdType.MESH
F32 = jnp.float32
BF16 = jnp.bfloat16

RING = 8
SEG = 128
RANK = 64
HALF = RANK // 2
SHORT = 384
PIECES = ((384, 256), (640, 384))
GROUPS = 128 // HALF
STEP = 3
ORDER = (2, 1, 3, 0)


def nt_dot(a, b):
    return lax.dot_general(a, b, (((1,), (1,)), ((), ())), preferred_element_type=F32)


def kernel(
    n_dp,
    n_tensor,
    tokens_hbm,
    w_hbm,
    down_hbm,
    up_hbm,
    slot_hbm,
    ids_hbm,
    live_hbm,
    out_ref,
    tok,
    tok_other,
    w,
    down,
    up,
    slot,
    ids,
    live,
    req_out,
    req_in,
    a_out,
    a_in,
    relay,
    b_out,
    b_in,
    mine,
    core_out,
    core_in,
    x_out,
    x_in,
    s_mine,
    s_out,
    s_in,
    s_all,
    acc,
    load_sem,
    req_send,
    req_recv,
    a_send,
    a_recv,
    swap_send,
    swap_recv,
    relay_send,
    relay_recv,
    pass_send,
    pass_recv,
    b_send,
    b_recv,
    core_send,
    core_recv,
    x_send,
    x_recv,
    s_send,
    s_recv,
):
    me = lax.axis_index("dp")
    t = lax.axis_index("tensor")
    n_chip = n_tensor // 2
    segs = tok.shape[0]
    stored = down.shape[0]

    core = lax.rem(t, 2)
    sides = (t, t + 1 - 2 * core)

    def dp_at(offset, cross=0):
        return (lax.rem(me + offset + n_dp, n_dp), sides[cross])

    def tensor_at(offset):
        return (me, lax.rem(t + offset, n_tensor))

    other_core = (me, sides[1])

    def far_relay(asker):
        return asker // RING * RING + lax.rem(lax.rem(asker, RING) + 5, RING)

    relay_to = (far_relay(lax.rem(me + n_dp - 3, n_dp)), t)
    pass_index = me // RING * RING + lax.rem(lax.rem(me, RING) + RING - 5, RING)
    pass_to = [(pass_index, side) for side in sides]

    def remote(src, dst, send, recv, device):
        return pltpu.make_async_remote_copy(
            src_ref=src, dst_ref=dst, send_sem=send, recv_sem=recv, device_id=device, device_id_type=MESH
        )

    barrier = pltpu.get_barrier_semaphore()
    peers = [dp_at(o) for o in (-1, -2, -3)] + [pass_to[0]]
    peers += [tensor_at(k) for k in range(1, n_tensor)]
    for peer in peers:
        pl.semaphore_signal(barrier, inc=1, device_id=peer, device_id_type=MESH)

    small = [
        pltpu.make_async_copy(src, dst, load_sem.at[i])
        for i, (src, dst) in enumerate(((slot_hbm, slot), (ids_hbm, ids), (live_hbm, live)))
    ]
    down_load = pltpu.make_async_copy(down_hbm, down, load_sem.at[3])
    up_load = pltpu.make_async_copy(up_hbm, up, load_sem.at[4])
    tok_load = pltpu.make_async_copy(tokens_hbm, tok, load_sem.at[5])
    w_load = []
    for i, k in enumerate(ORDER):
        for side in range(2):
            owner = lax.rem(t + 2 * k, n_tensor)
            if side:
                owner = owner + 1 - 2 * lax.rem(owner, 2)
            columns = pl.ds(pl.multiple_of(owner * 128, 128), 128)
            w_load.append(
                pltpu.make_async_copy(
                    w_hbm.at[:, columns], w.at[i, :, pl.ds(side * 128, 128)], load_sem.at[6 + 2 * i + side]
                )
            )
    for copy in small:
        copy.start()
    down_load.start()
    tok_load.start()
    for copy in w_load:
        copy.start()
    up_load.start()

    for copy in small:
        copy.wait()
    offs, locs = [], []
    for s in range(segs):
        place = slot[ids[s]]
        offs.append(lax.rem(place // stored - me + n_dp, n_dp))
        locs.append(lax.rem(place, stored))
    wanted = []
    for o in range(4):
        found = jnp.int32(0)
        for s in range(4):
            found = jnp.where(offs[s] == o, locs[s], found)
        wanted.append(found)
    far_seg = jnp.int32(0)
    for s in range(4):
        far_seg = jnp.where(offs[s] == 3, s, far_seg)
    live_count = live[0]
    for o in range(1, 4):
        req_out[o - 1] = jnp.full(req_out.shape[1:], wanted[o], jnp.int32)

    pl.semaphore_wait(barrier, len(peers))
    asks = [
        remote(req_out.at[o - 1], req_in.at[o - 1], req_send.at[o - 1], req_recv.at[o - 1], dp_at(o))
        for o in range(1, 4)
    ]
    for copy in asks:
        copy.start()

    core_copies, swap_copies, s_copies = [], [], []

    def rank_half(cross):
        start_row = (1 - core) * HALF if cross else core * HALF
        return pl.ds(pl.multiple_of(start_row, HALF), HALF)

    x_copies = [
        remote(x_out.at[i], x_in.at[i], x_send.at[i], x_recv.at[i], tensor_at(2 * ORDER[i])) for i in range(3)
    ]
    a_copies, b_copies, relay_copies, pass_copies = [], [], [], []
    for o in range(1, 4):
        for cross in range(2):
            lanes = pl.ds(0, a_out.shape[2] if o < 3 else SHORT)
            n = 2 * (o - 1) + cross
            src = a_out.at[o, rank_half(cross), lanes]
            a_copies.append(remote(src, a_in.at[o, cross, :, lanes], a_send.at[n], a_recv.at[n], dp_at(-o, cross)))
        b_copies.append(remote(b_out.at[o - 1], b_in.at[o], b_send.at[o - 1], b_recv.at[o - 1], dp_at(-o)))
    for p, (first, size) in enumerate(PIECES):
        for cross in range(2):
            n = 2 * p + cross
            src = a_out.at[3, rank_half(cross), pl.ds(first, size)]
            here = relay.at[cross, :, pl.ds(first - SHORT, size)]
            dst = a_in.at[3, cross, :, pl.ds(first, size)]
            relay_copies.append(remote(src, here, relay_send.at[n], relay_recv.at[n], relay_to))
            pass_copies.append(remote(here, dst, pass_send.at[n], pass_recv.at[n], pass_to[cross]))

    def base_block(i):
        w_load[2 * i].wait()
        w_load[2 * i + 1].wait()
        for s in range(0, segs, STEP):
            rows = tok[pl.ds(s, STEP)].reshape(STEP * SEG, tok.shape[2])
            part = jnp.dot(rows, w[i], preferred_element_type=F32)
            mine[i, pl.ds(s * SEG, STEP * SEG), :] = part[:, :128]
            core_out[i, pl.ds(s * SEG, STEP * SEG), :] = part[:, 128:]
        copy = remote(core_out.at[i], core_in.at[i], core_send.at[i], core_recv.at[i], other_core)
        copy.start()
        core_copies.append(copy)

    def base_send(i):
        core_copies[i].wait_recv()
        x_out[i] = (mine[i] + core_in[i]).astype(BF16)
        x_copies[i].start()

    def pick(o):
        asks[o - 1].wait_recv()
        asked = jnp.max(req_in[o - 1])
        a_out[o] = down[asked]
        b_out[o - 1] = up[asked]

    def give(o, *crosses):
        for cross in crosses:
            a_copies[2 * (o - 1) + cross].start()

    def serve(o):
        pick(o)
        if o == 3:
            for copy in relay_copies:
                copy.start()
        give(o, 0, 1)
        b_copies[o - 1].start()

    def pass_on():
        for there, onward in zip(relay_copies, pass_copies):
            there.wait_recv()
            onward.start()

    def serve_all():
        pick(1)
        give(1, 0)
        pick(2)
        give(2, 0)
        pick(3)
        for copy in relay_copies:
            copy.start()
        give(3, 0, 1)
        give(2, 1)
        give(1, 1)
        for copy in b_copies:
            copy.start()
        base_send(1)
        base_send(2)
        swap()
        pass_on()

    def serve_within(near):
        for o in range(1, 1 + near):
            serve(o)
        base_send(1)
        base_send(2)
        swap()
        pass_on()
        for o in range(1 + near, 4):
            serve(o)

    def swap():
        for copy in swap_copies:
            copy.start()

    tok_load.wait()
    base_block(0)
    base_block(1)
    down_load.wait()
    up_load.wait()
    a_out[0] = down[wanted[0]]
    a_in[0, 0] = a_out[0, rank_half(0)]
    b_in[0] = up[wanted[0]]
    base_block(2)
    base_block(3)
    base_send(0)
    swap_copies.append(remote(tok, tok_other, swap_send.at[0], swap_recv.at[0], other_core))
    swap_copies.append(remote(a_out.at[0, rank_half(1)], a_in.at[0, 1], swap_send.at[1], swap_recv.at[1], other_core))

    @pl.when(me > 2)
    def _():
        serve_all()

    for near in range(3):

        @pl.when(me == near)
        def _():
            serve_within(near)

    lane_group = lax.broadcasted_iota(jnp.int32, (SEG, 128), 1) // HALF
    row_group = lax.broadcasted_iota(jnp.int32, (SEG, 128), 0) // HALF
    own_group = lane_group == row_group

    def spread(a):
        return jnp.concatenate([a] * GROUPS, axis=0)

    for copy in swap_copies + a_copies + pass_copies:
        copy.wait_recv()
    for s in range(segs):
        o = jnp.minimum(offs[s], 3)
        part = nt_dot(tok[s], spread(a_in[o, 0])) + nt_dot(tok_other[s], spread(a_in[o, 1]))
        kept = jnp.where(own_group, part, 0.0)
        packed = kept[:HALF]
        for g in range(1, GROUPS):
            packed = packed + kept[g * HALF : (g + 1) * HALF]
        s_mine[s] = packed
        s_out[s] = packed.astype(BF16)
    for k in range(1, n_chip):
        copy = remote(s_out, s_in.at[k - 1], s_send.at[k - 1], s_recv.at[k - 1], tensor_at(2 * k))
        copy.start()
        s_copies.append(copy)


    core_copies[3].wait_recv()
    for copy in x_copies:
        copy.wait_recv()
    acc[...] = mine[3] + core_in[3] + x_in[0].astype(F32) + x_in[1].astype(F32) + x_in[2].astype(F32)

    for copy in s_copies:
        copy.wait_recv()
    total = s_mine[...]
    for k in range(n_chip - 1):
        total = total + s_in[k].astype(F32)
    s_all[core] = total.astype(BF16)
    copy = remote(s_all.at[core], s_all.at[core], s_send.at[n_chip - 1], s_recv.at[n_chip - 1], other_core)
    copy.start()
    s_copies.append(copy)

    for copy in b_copies:
        copy.wait_recv()
    s_copies[-1].wait_recv()
    for s in range(segs):
        factor = b_in[jnp.minimum(offs[s], 3)]
        add = None
        for h in range(2):
            x = jnp.where(own_group, spread(s_all[h, s].astype(F32)), 0.0).astype(BF16)
            term = jnp.dot(x, spread(factor[h * HALF : (h + 1) * HALF]), preferred_element_type=F32)
            add = term if add is None else add + term
        add = jnp.where(s < live_count, add, 0.0)
        rows = pl.ds(s * SEG, SEG)
        out_ref[rows, :] = (acc[rows, :] + add).astype(out_ref.dtype)

    for copy in asks + a_copies + swap_copies + relay_copies + pass_copies + b_copies + core_copies + x_copies + s_copies:
        copy.wait_send()


def per_device(n_dp, n_tensor, tokens, w, down, up, slot, ids, live):
    rows, width = tokens.shape
    segs = ids.shape[0]
    stored, rank, columns = up.shape
    chips = n_tensor // 2
    dma = pltpu.SemaphoreType.DMA
    vmem, smem = pltpu.VMEM, pltpu.SMEM
    return pl.pallas_call(
        functools.partial(kernel, n_dp, n_tensor),
        name="adapted_projection",
        out_shape=pltpu.VMEM((rows, columns), BF16),
        in_specs=[pl.BlockSpec(memory_space=pl.ANY)] * 7,
        out_specs=pl.BlockSpec(memory_space=pltpu.VMEM),
        scratch_shapes=[
            vmem((segs, SEG, width), BF16),
            vmem((segs, SEG, width), BF16),
            vmem((4, width, 2 * columns), BF16),
            vmem((stored, rank, width), BF16),
            vmem((stored, rank, columns), BF16),
            smem(slot.shape, jnp.int32),
            smem(ids.shape, jnp.int32),
            smem(live.shape, jnp.int32),
            vmem((3, 8, 128), jnp.int32),
            vmem((3, 8, 128), jnp.int32),
            vmem((4, rank, width), BF16),
            vmem((4, 2, HALF, width), BF16),
            vmem((2, HALF, width - SHORT), BF16),
            vmem((3, rank, columns), BF16),
            vmem((4, rank, columns), BF16),
            vmem((4, rows, columns), F32),
            vmem((4, rows, columns), F32),
            vmem((4, rows, columns), F32),
            vmem((3, rows, columns), BF16),
            vmem((3, rows, columns), BF16),
            vmem((segs, HALF, 128), F32),
            vmem((segs, HALF, 128), BF16),
            vmem((chips - 1, segs, HALF, 128), BF16),
            vmem((2, segs, HALF, 128), BF16),
            vmem((rows, columns), F32),
            dma((14,)),
            dma((3,)),
            dma((3,)),
            dma((6,)),
            dma((6,)),
            dma((2,)),
            dma((2,)),
            dma((2 * len(PIECES),)),
            dma((2 * len(PIECES),)),
            dma((2 * len(PIECES),)),
            dma((2 * len(PIECES),)),
            dma((3,)),
            dma((3,)),
            dma((4,)),
            dma((4,)),
            dma((3,)),
            dma((3,)),
            dma((chips,)),
            dma((chips,)),
        ],
        compiler_params=pltpu.CompilerParams(
            collective_id=0, has_side_effects=True, vmem_limit_bytes=63 * 1024 * 1024
        ),
        cost_estimate=pl.CostEstimate(flops=2_000_000_000, bytes_accessed=4_500_000, transcendentals=0),
    )(tokens.reshape(segs, SEG, width), w, down, up, slot, ids, live)


def solution(mesh):
    placed = (
        P("dp", "tensor"),
        P("tensor", None),
        P("dp", None, "tensor"),
        P("dp", None, "tensor"),
        P(),
        P("dp"),
        P("dp"),
    )
    return jax.shard_map(
        functools.partial(per_device, mesh.shape["dp"], mesh.shape["tensor"]),
        mesh=mesh,
        in_specs=placed,
        out_specs=P("dp", "tensor"),
        check_vma=False,
    )
```

```python
import functools

import jax
import jax.numpy as jnp
from jax import lax
from jax.experimental import pallas as pl
from jax.experimental.pallas import tpu as pltpu
from jax.sharding import PartitionSpec as P

MESH = pl.DeviceIdType.MESH
F32 = jnp.float32
BF16 = jnp.bfloat16

RING = 8
SEG = 128
RANK = 64
HALF = RANK // 2
SHORT = 384
PIECES = ((384, 256), (640, 384))
GROUPS = 128 // HALF
STEP = 3
ORDER = (2, 1, 3, 0)


def nt_dot(a, b):
    return lax.dot_general(a, b, (((1,), (1,)), ((), ())), preferred_element_type=F32)


def kernel(
    n_dp,
    n_tensor,
    tokens_hbm,
    w_hbm,
    down_hbm,
    up_hbm,
    slot_hbm,
    ids_hbm,
    live_hbm,
    out_ref,
    tok,
    tok_other,
    w,
    down,
    up,
    slot,
    ids,
    live,
    req_out,
    req_in,
    a_out,
    a_in,
    relay,
    b_out,
    b_in,
    mine,
    core_out,
    core_in,
    x_out,
    x_in,
    s_mine,
    s_out,
    s_in,
    s_all,
    acc,
    load_sem,
    req_send,
    req_recv,
    a_send,
    a_recv,
    swap_send,
    swap_recv,
    relay_send,
    relay_recv,
    pass_send,
    pass_recv,
    b_send,
    b_recv,
    core_send,
    core_recv,
    x_send,
    x_recv,
    s_send,
    s_recv,
):
    me = lax.axis_index("dp")
    t = lax.axis_index("tensor")
    n_chip = n_tensor // 2
    segs = tok.shape[0]
    stored = down.shape[0]

    core = lax.rem(t, 2)
    sides = (t, t + 1 - 2 * core)

    def dp_at(offset, cross=0):
        return (lax.rem(me + offset + n_dp, n_dp), sides[cross])

    def tensor_at(offset):
        return (me, lax.rem(t + offset, n_tensor))

    other_core = (me, sides[1])

    def far_relay(asker):
        return asker // RING * RING + lax.rem(lax.rem(asker, RING) + 5, RING)

    relay_to = (far_relay(lax.rem(me + n_dp - 3, n_dp)), t)
    pass_index = me // RING * RING + lax.rem(lax.rem(me, RING) + RING - 5, RING)
    pass_to = [(pass_index, side) for side in sides]

    def remote(src, dst, send, recv, device):
        return pltpu.make_async_remote_copy(
            src_ref=src, dst_ref=dst, send_sem=send, recv_sem=recv, device_id=device, device_id_type=MESH
        )

    barrier = pltpu.get_barrier_semaphore()
    peers = [dp_at(o) for o in (-1, -2, -3)] + [pass_to[0]]
    peers += [tensor_at(k) for k in range(1, n_tensor)]
    for peer in peers:
        pl.semaphore_signal(barrier, inc=1, device_id=peer, device_id_type=MESH)

    small = [
        pltpu.make_async_copy(src, dst, load_sem.at[i])
        for i, (src, dst) in enumerate(((slot_hbm, slot), (ids_hbm, ids), (live_hbm, live)))
    ]
    down_load = pltpu.make_async_copy(down_hbm, down, load_sem.at[3])
    up_load = pltpu.make_async_copy(up_hbm, up, load_sem.at[4])
    tok_load = pltpu.make_async_copy(tokens_hbm, tok, load_sem.at[5])
    w_load = []
    for i, k in enumerate(ORDER):
        for side in range(2):
            owner = lax.rem(t + 2 * k, n_tensor)
            if side:
                owner = owner + 1 - 2 * lax.rem(owner, 2)
            columns = pl.ds(pl.multiple_of(owner * 128, 128), 128)
            w_load.append(
                pltpu.make_async_copy(
                    w_hbm.at[:, columns], w.at[i, :, pl.ds(side * 128, 128)], load_sem.at[6 + 2 * i + side]
                )
            )
    for copy in small:
        copy.start()
    down_load.start()
    tok_load.start()
    for copy in w_load:
        copy.start()
    up_load.start()

    for copy in small:
        copy.wait()
    offs, locs = [], []
    for s in range(segs):
        place = slot[ids[s]]
        offs.append(lax.rem(place // stored - me + n_dp, n_dp))
        locs.append(lax.rem(place, stored))
    wanted = []
    for o in range(4):
        found = jnp.int32(0)
        for s in range(4):
            found = jnp.where(offs[s] == o, locs[s], found)
        wanted.append(found)
    far_seg = jnp.int32(0)
    for s in range(4):
        far_seg = jnp.where(offs[s] == 3, s, far_seg)
    live_count = live[0]
    for o in range(1, 4):
        req_out[o - 1] = jnp.full(req_out.shape[1:], wanted[o], jnp.int32)

    pl.semaphore_wait(barrier, len(peers))
    asks = [
        remote(req_out.at[o - 1], req_in.at[o - 1], req_send.at[o - 1], req_recv.at[o - 1], dp_at(o))
        for o in range(1, 4)
    ]
    for copy in asks:
        copy.start()

    core_copies, swap_copies, s_copies = [], [], []

    def rank_half(cross):
        start_row = (1 - core) * HALF if cross else core * HALF
        return pl.ds(pl.multiple_of(start_row, HALF), HALF)

    x_copies = [
        remote(x_out.at[i], x_in.at[i], x_send.at[i], x_recv.at[i], tensor_at(2 * ORDER[i])) for i in range(3)
    ]
    a_copies, b_copies, relay_copies, pass_copies = [], [], [], []
    for o in range(1, 4):
        for cross in range(2):
            lanes = pl.ds(0, a_out.shape[2] if o < 3 else SHORT)
            n = 2 * (o - 1) + cross
            src = a_out.at[o, rank_half(cross), lanes]
            a_copies.append(remote(src, a_in.at[o, cross, :, lanes], a_send.at[n], a_recv.at[n], dp_at(-o, cross)))
        b_copies.append(remote(b_out.at[o - 1], b_in.at[o], b_send.at[o - 1], b_recv.at[o - 1], dp_at(-o)))
    for p, (first, size) in enumerate(PIECES):
        for cross in range(2):
            n = 2 * p + cross
            src = a_out.at[3, rank_half(cross), pl.ds(first, size)]
            here = relay.at[cross, :, pl.ds(first - SHORT, size)]
            dst = a_in.at[3, cross, :, pl.ds(first, size)]
            relay_copies.append(remote(src, here, relay_send.at[n], relay_recv.at[n], relay_to))
            pass_copies.append(remote(here, dst, pass_send.at[n], pass_recv.at[n], pass_to[cross]))

    def base_block(i):
        w_load[2 * i].wait()
        w_load[2 * i + 1].wait()
        for s in range(0, segs, STEP):
            rows = tok[pl.ds(s, STEP)].reshape(STEP * SEG, tok.shape[2])
            part = jnp.dot(rows, w[i], preferred_element_type=F32)
            mine[i, pl.ds(s * SEG, STEP * SEG), :] = part[:, :128]
            core_out[i, pl.ds(s * SEG, STEP * SEG), :] = part[:, 128:]
        copy = remote(core_out.at[i], core_in.at[i], core_send.at[i], core_recv.at[i], other_core)
        copy.start()
        core_copies.append(copy)

    def base_send(i):
        core_copies[i].wait_recv()
        x_out[i] = (mine[i] + core_in[i]).astype(BF16)
        x_copies[i].start()

    def pick(o):
        asks[o - 1].wait_recv()
        asked = jnp.max(req_in[o - 1])
        a_out[o] = down[asked]
        b_out[o - 1] = up[asked]

    def give(o, *crosses):
        for cross in crosses:
            a_copies[2 * (o - 1) + cross].start()

    def pass_on():
        for there, onward in zip(relay_copies, pass_copies):
            there.wait_recv()
            onward.start()

    def serve(near):
        late = range(near + 1, 4)
        for o in late:
            pick(o)
            if o < 3:
                give(o, 0)
        for copy in relay_copies:
            copy.start()
        give(3, 0, 1)
        for o in reversed(late):
            if o < 3:
                give(o, 1)
        for o in late:
            b_copies[o - 1].start()

    def serve_all():
        pick(1)
        give(1, 0)
        pick(2)
        give(2, 0)
        pick(3)
        for copy in relay_copies:
            copy.start()
        give(3, 0, 1)
        give(2, 1)
        give(1, 1)
        for copy in b_copies:
            copy.start()
        base_send(1)
        base_send(2)
        swap()
        pass_on()

    def serve_within(near):
        for o in range(1, 1 + near):
            pick(o)
            give(o, 0, 1)
            b_copies[o - 1].start()
        base_send(1)
        base_send(2)
        swap()
        pass_on()
        serve(near)

    def swap():
        for copy in swap_copies:
            copy.start()

    tok_load.wait()
    base_block(0)
    base_block(1)
    down_load.wait()
    up_load.wait()
    a_out[0] = down[wanted[0]]
    a_in[0, 0] = a_out[0, rank_half(0)]
    b_in[0] = up[wanted[0]]
    base_block(2)
    base_block(3)
    base_send(0)
    swap_copies.append(remote(tok, tok_other, swap_send.at[0], swap_recv.at[0], other_core))
    swap_copies.append(remote(a_out.at[0, rank_half(1)], a_in.at[0, 1], swap_send.at[1], swap_recv.at[1], other_core))

    @pl.when(me > 2)
    def _():
        serve_all()

    for near in range(3):

        @pl.when(me == near)
        def _():
            serve_within(near)

    lane_group = lax.broadcasted_iota(jnp.int32, (SEG, 128), 1) // HALF
    row_group = lax.broadcasted_iota(jnp.int32, (SEG, 128), 0) // HALF
    own_group = lane_group == row_group

    def spread(a):
        return jnp.concatenate([a] * GROUPS, axis=0)

    for copy in swap_copies + a_copies + pass_copies:
        copy.wait_recv()
    for s in range(segs):
        o = jnp.minimum(offs[s], 3)
        part = nt_dot(tok[s], spread(a_in[o, 0])) + nt_dot(tok_other[s], spread(a_in[o, 1]))
        kept = jnp.where(own_group, part, 0.0)
        packed = kept[:HALF]
        for g in range(1, GROUPS):
            packed = packed + kept[g * HALF : (g + 1) * HALF]
        s_mine[s] = packed
        s_out[s] = packed.astype(BF16)
    for k in range(1, n_chip):
        copy = remote(s_out, s_in.at[k - 1], s_send.at[k - 1], s_recv.at[k - 1], tensor_at(2 * k))
        copy.start()
        s_copies.append(copy)


    core_copies[3].wait_recv()
    for copy in x_copies:
        copy.wait_recv()
    acc[...] = mine[3] + core_in[3] + x_in[0].astype(F32) + x_in[1].astype(F32) + x_in[2].astype(F32)

    for copy in s_copies:
        copy.wait_recv()
    total = s_mine[...]
    for k in range(n_chip - 1):
        total = total + s_in[k].astype(F32)
    s_all[core] = total.astype(BF16)
    copy = remote(s_all.at[core], s_all.at[core], s_send.at[n_chip - 1], s_recv.at[n_chip - 1], other_core)
    copy.start()
    s_copies.append(copy)

    for copy in b_copies:
        copy.wait_recv()
    s_copies[-1].wait_recv()
    for s in range(segs):
        factor = b_in[jnp.minimum(offs[s], 3)]
        add = None
        for h in range(2):
            x = jnp.where(own_group, spread(s_all[h, s].astype(F32)), 0.0).astype(BF16)
            term = jnp.dot(x, spread(factor[h * HALF : (h + 1) * HALF]), preferred_element_type=F32)
            add = term if add is None else add + term
        add = jnp.where(s < live_count, add, 0.0)
        rows = pl.ds(s * SEG, SEG)
        out_ref[rows, :] = (acc[rows, :] + add).astype(out_ref.dtype)

    for copy in asks + a_copies + swap_copies + relay_copies + pass_copies + b_copies + core_copies + x_copies + s_copies:
        copy.wait_send()


def per_device(n_dp, n_tensor, tokens, w, down, up, slot, ids, live):
    rows, width = tokens.shape
    segs = ids.shape[0]
    stored, rank, columns = up.shape
    chips = n_tensor // 2
    dma = pltpu.SemaphoreType.DMA
    vmem, smem = pltpu.VMEM, pltpu.SMEM
    return pl.pallas_call(
        functools.partial(kernel, n_dp, n_tensor),
        name="adapted_projection",
        out_shape=pltpu.VMEM((rows, columns), BF16),
        in_specs=[pl.BlockSpec(memory_space=pl.ANY)] * 7,
        out_specs=pl.BlockSpec(memory_space=pltpu.VMEM),
        scratch_shapes=[
            vmem((segs, SEG, width), BF16),
            vmem((segs, SEG, width), BF16),
            vmem((4, width, 2 * columns), BF16),
            vmem((stored, rank, width), BF16),
            vmem((stored, rank, columns), BF16),
            smem(slot.shape, jnp.int32),
            smem(ids.shape, jnp.int32),
            smem(live.shape, jnp.int32),
            vmem((3, 8, 128), jnp.int32),
            vmem((3, 8, 128), jnp.int32),
            vmem((4, rank, width), BF16),
            vmem((4, 2, HALF, width), BF16),
            vmem((2, HALF, width - SHORT), BF16),
            vmem((3, rank, columns), BF16),
            vmem((4, rank, columns), BF16),
            vmem((4, rows, columns), F32),
            vmem((4, rows, columns), F32),
            vmem((4, rows, columns), F32),
            vmem((3, rows, columns), BF16),
            vmem((3, rows, columns), BF16),
            vmem((segs, HALF, 128), F32),
            vmem((segs, HALF, 128), BF16),
            vmem((chips - 1, segs, HALF, 128), BF16),
            vmem((2, segs, HALF, 128), BF16),
            vmem((rows, columns), F32),
            dma((14,)),
            dma((3,)),
            dma((3,)),
            dma((6,)),
            dma((6,)),
            dma((2,)),
            dma((2,)),
            dma((2 * len(PIECES),)),
            dma((2 * len(PIECES),)),
            dma((2 * len(PIECES),)),
            dma((2 * len(PIECES),)),
            dma((3,)),
            dma((3,)),
            dma((4,)),
            dma((4,)),
            dma((3,)),
            dma((3,)),
            dma((chips,)),
            dma((chips,)),
        ],
        compiler_params=pltpu.CompilerParams(
            collective_id=0, has_side_effects=True, vmem_limit_bytes=63 * 1024 * 1024
        ),
        cost_estimate=pl.CostEstimate(flops=2_000_000_000, bytes_accessed=4_500_000, transcendentals=0),
    )(tokens.reshape(segs, SEG, width), w, down, up, slot, ids, live)


def solution(mesh):
    placed = (
        P("dp", "tensor"),
        P("tensor", None),
        P("dp", None, "tensor"),
        P("dp", None, "tensor"),
        P(),
        P("dp"),
        P("dp"),
    )
    return jax.shard_map(
        functools.partial(per_device, mesh.shape["dp"], mesh.shape["tensor"]),
        mesh=mesh,
        in_specs=placed,
        out_specs=P("dp", "tensor"),
        check_vma=False,
    )
```

```python
import functools

import jax
import jax.numpy as jnp
from jax import lax
from jax.experimental import pallas as pl
from jax.experimental.pallas import tpu as pltpu
from jax.sharding import PartitionSpec as P

MESH = pl.DeviceIdType.MESH
F32 = jnp.float32
BF16 = jnp.bfloat16

RING = 8
SEG = 128
RANK = 64
HALF = RANK // 2
SHORT = 384
PIECES = ((384, 256), (640, 384))
GROUPS = 128 // HALF
CHUNKS = 3
STEP = 3
ORDER = (2, 1, 3, 0)


def nt_dot(a, b):
    return lax.dot_general(a, b, (((1,), (1,)), ((), ())), preferred_element_type=F32)


def kernel(
    n_dp,
    n_tensor,
    tokens_hbm,
    w_hbm,
    down_hbm,
    up_hbm,
    slot_hbm,
    ids_hbm,
    live_hbm,
    out_ref,
    tok,
    tok_other,
    w,
    down,
    up,
    slot,
    ids,
    live,
    req_out,
    req_in,
    a_out,
    a_in,
    relay,
    b_out,
    b_in,
    mine,
    core_out,
    core_in,
    x_out,
    x_in,
    s_mine,
    s_out,
    s_in,
    s_all,
    acc,
    load_sem,
    req_send,
    req_recv,
    a_send,
    a_recv,
    swap_send,
    swap_recv,
    relay_send,
    relay_recv,
    pass_send,
    pass_recv,
    b_send,
    b_recv,
    core_send,
    core_recv,
    x_send,
    x_recv,
    s_send,
    s_recv,
):
    me = lax.axis_index("dp")
    t = lax.axis_index("tensor")
    n_chip = n_tensor // 2
    segs = tok.shape[0]
    stored = down.shape[0]

    core = lax.rem(t, 2)
    sides = (t, t + 1 - 2 * core)

    def dp_at(offset, cross=0):
        return (lax.rem(me + offset + n_dp, n_dp), sides[cross])

    def tensor_at(offset):
        return (me, lax.rem(t + offset, n_tensor))

    other_core = (me, sides[1])

    def far_relay(asker):
        return asker // RING * RING + lax.rem(lax.rem(asker, RING) + 5, RING)

    relay_to = (far_relay(lax.rem(me + n_dp - 3, n_dp)), t)
    pass_index = me // RING * RING + lax.rem(lax.rem(me, RING) + RING - 5, RING)
    pass_to = [(pass_index, side) for side in sides]

    def remote(src, dst, send, recv, device):
        return pltpu.make_async_remote_copy(
            src_ref=src, dst_ref=dst, send_sem=send, recv_sem=recv, device_id=device, device_id_type=MESH
        )

    barrier = pltpu.get_barrier_semaphore()
    peers = [dp_at(o) for o in (-1, -2, -3)] + [pass_to[0]]
    peers += [tensor_at(k) for k in range(1, n_tensor)]
    for peer in peers:
        pl.semaphore_signal(barrier, inc=1, device_id=peer, device_id_type=MESH)

    small = [
        pltpu.make_async_copy(src, dst, load_sem.at[i])
        for i, (src, dst) in enumerate(((slot_hbm, slot), (ids_hbm, ids), (live_hbm, live)))
    ]
    down_load = pltpu.make_async_copy(down_hbm, down, load_sem.at[3])
    up_load = pltpu.make_async_copy(up_hbm, up, load_sem.at[4])
    tok_load = pltpu.make_async_copy(tokens_hbm, tok, load_sem.at[5])
    w_load = []
    for i, k in enumerate(ORDER):
        for side in range(2):
            owner = lax.rem(t + 2 * k, n_tensor)
            if side:
                owner = owner + 1 - 2 * lax.rem(owner, 2)
            columns = pl.ds(pl.multiple_of(owner * 128, 128), 128)
            w_load.append(
                pltpu.make_async_copy(
                    w_hbm.at[:, columns], w.at[i, :, pl.ds(side * 128, 128)], load_sem.at[6 + 2 * i + side]
                )
            )
    for copy in small:
        copy.start()
    down_load.start()
    tok_load.start()
    for copy in w_load:
        copy.start()
    up_load.start()

    for copy in small:
        copy.wait()
    offs, locs = [], []
    for s in range(segs):
        place = slot[ids[s]]
        offs.append(lax.rem(place // stored - me + n_dp, n_dp))
        locs.append(lax.rem(place, stored))
    wanted = []
    for o in range(4):
        found = jnp.int32(0)
        for s in range(4):
            found = jnp.where(offs[s] == o, locs[s], found)
        wanted.append(found)
    far_seg = jnp.int32(0)
    for s in range(4):
        far_seg = jnp.where(offs[s] == 3, s, far_seg)
    live_count = live[0]
    for o in range(1, 4):
        req_out[o - 1] = jnp.full(req_out.shape[1:], wanted[o], jnp.int32)

    pl.semaphore_wait(barrier, len(peers))
    asks = [
        remote(req_out.at[o - 1], req_in.at[o - 1], req_send.at[o - 1], req_recv.at[o - 1], dp_at(o))
        for o in range(1, 4)
    ]
    for copy in asks:
        copy.start()

    core_copies, swap_copies, s_copies = [], [], []

    def rank_half(cross):
        start_row = (1 - core) * HALF if cross else core * HALF
        return pl.ds(pl.multiple_of(start_row, HALF), HALF)

    x_copies = [
        remote(x_out.at[i], x_in.at[i], x_send.at[i], x_recv.at[i], tensor_at(2 * ORDER[i])) for i in range(3)
    ]
    a_copies, b_copies, relay_copies, pass_copies = [], [], [], []
    for o in range(1, 4):
        for cross in range(2):
            lanes = pl.ds(0, a_out.shape[2] if o < 3 else SHORT)
            n = 2 * (o - 1) + cross
            src = a_out.at[o, rank_half(cross), lanes]
            a_copies.append(remote(src, a_in.at[o, cross, :, lanes], a_send.at[n], a_recv.at[n], dp_at(-o, cross)))
        b_copies.append(remote(b_out.at[o - 1], b_in.at[o], b_send.at[o - 1], b_recv.at[o - 1], dp_at(-o)))
    for p, (first, size) in enumerate(PIECES):
        for cross in range(2):
            n = 2 * p + cross
            src = a_out.at[3, rank_half(cross), pl.ds(first, size)]
            here = relay.at[cross, :, pl.ds(first - SHORT, size)]
            dst = a_in.at[3, cross, :, pl.ds(first, size)]
            relay_copies.append(remote(src, here, relay_send.at[n], relay_recv.at[n], relay_to))
            pass_copies.append(remote(here, dst, pass_send.at[n], pass_recv.at[n], pass_to[cross]))

    def base_block(i):
        w_load[2 * i].wait()
        w_load[2 * i + 1].wait()
        for s in range(0, segs, STEP):
            rows = tok[pl.ds(s, STEP)].reshape(STEP * SEG, tok.shape[2])
            part = jnp.dot(rows, w[i], preferred_element_type=F32)
            mine[i, pl.ds(s * SEG, STEP * SEG), :] = part[:, :128]
            core_out[i, pl.ds(s * SEG, STEP * SEG), :] = part[:, 128:]
        copy = remote(core_out.at[i], core_in.at[i], core_send.at[i], core_recv.at[i], other_core)
        copy.start()
        core_copies.append(copy)

    def base_send(i):
        core_copies[i].wait_recv()
        x_out[i] = (mine[i] + core_in[i]).astype(BF16)
        x_copies[i].start()

    def pick(o):
        asks[o - 1].wait_recv()
        asked = jnp.max(req_in[o - 1])
        a_out[o] = down[asked]
        b_out[o - 1] = up[asked]

    def give(o, *crosses):
        for cross in crosses:
            a_copies[2 * (o - 1) + cross].start()

    def pass_on():
        for there, onward in zip(relay_copies, pass_copies):
            there.wait_recv()
            onward.start()

    def serve(near):
        late = range(near + 1, 4)
        for o in late:
            pick(o)
            if o < 3:
                give(o, 0)
        for copy in relay_copies:
            copy.start()
        give(3, 0, 1)
        for o in reversed(late):
            if o < 3:
                give(o, 1)
        for o in late:
            b_copies[o - 1].start()

    def serve_all():
        pick(1)
        give(1, 0)
        pick(2)
        give(2, 0)
        pick(3)
        for copy in relay_copies:
            copy.start()
        give(3, 0, 1)
        give(2, 1)
        give(1, 1)
        for copy in b_copies:
            copy.start()
        base_send(1)
        base_send(2)
        swap()
        pass_on()

    def serve_within(near):
        for o in range(1, 1 + near):
            pick(o)
            give(o, 0, 1)
            b_copies[o - 1].start()
        base_send(1)
        base_send(2)
        swap()
        pass_on()
        serve(near)

    def swap():
        for copy in swap_copies:
            copy.start()

    tok_load.wait()
    base_block(0)
    base_block(1)
    down_load.wait()
    up_load.wait()
    a_out[0] = down[wanted[0]]
    a_in[0, 0] = a_out[0, rank_half(0)]
    b_in[0] = up[wanted[0]]
    base_block(2)
    base_block(3)
    base_send(0)
    swap_copies.append(remote(tok, tok_other, swap_send.at[0], swap_recv.at[0], other_core))
    swap_copies.append(remote(a_out.at[0, rank_half(1)], a_in.at[0, 1], swap_send.at[1], swap_recv.at[1], other_core))

    @pl.when(me > 2)
    def _():
        serve_all()

    for near in range(3):

        @pl.when(me == near)
        def _():
            serve_within(near)

    lane_group = lax.broadcasted_iota(jnp.int32, (SEG, 128), 1) // HALF
    row_group = lax.broadcasted_iota(jnp.int32, (SEG, 128), 0) // HALF
    own_group = lane_group == row_group

    def spread(a):
        return jnp.concatenate([a] * GROUPS, axis=0)

    for copy in swap_copies + a_copies + pass_copies:
        copy.wait_recv()
    chunk = segs // CHUNKS
    parts = [pl.ds(h * chunk, chunk) for h in range(CHUNKS)]
    sums = [[] for _ in parts]
    for h, part in enumerate(parts):
        for s in range(h * chunk, (h + 1) * chunk):
            o = jnp.minimum(offs[s], 3)
            both = nt_dot(tok[s], spread(a_in[o, 0])) + nt_dot(tok_other[s], spread(a_in[o, 1]))
            kept = jnp.where(own_group, both, 0.0)
            packed = kept[:HALF]
            for g in range(1, GROUPS):
                packed = packed + kept[g * HALF : (g + 1) * HALF]
            s_mine[s] = packed
            s_out[s] = packed.astype(BF16)
        for k in ORDER[:3]:
            n = h * n_chip + k
            copy = remote(s_out.at[part], s_in.at[k - 1, part], s_send.at[n], s_recv.at[n], tensor_at(2 * k))
            copy.start()
            sums[h].append(copy)

    core_copies[3].wait_recv()
    for copy in x_copies:
        copy.wait_recv()
    acc[...] = mine[3] + core_in[3] + x_in[0].astype(F32) + x_in[1].astype(F32) + x_in[2].astype(F32)

    for h, part in enumerate(parts):
        for copy in sums[h]:
            copy.wait_recv()
        total = s_mine[part]
        for k in range(n_chip - 1):
            total = total + s_in[k, part].astype(F32)
        s_all[core, part] = total.astype(BF16)
        mine_part = s_all.at[core, part]
        copy = remote(mine_part, mine_part, s_send.at[h * n_chip], s_recv.at[h * n_chip], other_core)
        copy.start()
        s_copies.append(copy)

    for copy in b_copies:
        copy.wait_recv()
    for s in range(segs):
        if s % chunk == 0:
            s_copies[s // chunk].wait_recv()
        factor = b_in[jnp.minimum(offs[s], 3)]
        add = None
        for h in range(2):
            x = jnp.where(own_group, spread(s_all[h, s].astype(F32)), 0.0).astype(BF16)
            term = jnp.dot(x, spread(factor[h * HALF : (h + 1) * HALF]), preferred_element_type=F32)
            add = term if add is None else add + term
        add = jnp.where(s < live_count, add, 0.0)
        rows = pl.ds(s * SEG, SEG)
        out_ref[rows, :] = (acc[rows, :] + add).astype(out_ref.dtype)

    for copy in asks + a_copies + swap_copies + relay_copies + pass_copies + b_copies + core_copies + x_copies + s_copies + sum(sums, []):
        copy.wait_send()


def per_device(n_dp, n_tensor, tokens, w, down, up, slot, ids, live):
    rows, width = tokens.shape
    segs = ids.shape[0]
    stored, rank, columns = up.shape
    chips = n_tensor // 2
    dma = pltpu.SemaphoreType.DMA
    vmem, smem = pltpu.VMEM, pltpu.SMEM
    return pl.pallas_call(
        functools.partial(kernel, n_dp, n_tensor),
        name="adapted_projection",
        out_shape=pltpu.VMEM((rows, columns), BF16),
        in_specs=[pl.BlockSpec(memory_space=pl.ANY)] * 7,
        out_specs=pl.BlockSpec(memory_space=pltpu.VMEM),
        scratch_shapes=[
            vmem((segs, SEG, width), BF16),
            vmem((segs, SEG, width), BF16),
            vmem((4, width, 2 * columns), BF16),
            vmem((stored, rank, width), BF16),
            vmem((stored, rank, columns), BF16),
            smem(slot.shape, jnp.int32),
            smem(ids.shape, jnp.int32),
            smem(live.shape, jnp.int32),
            vmem((3, 8, 128), jnp.int32),
            vmem((3, 8, 128), jnp.int32),
            vmem((4, rank, width), BF16),
            vmem((4, 2, HALF, width), BF16),
            vmem((2, HALF, width - SHORT), BF16),
            vmem((3, rank, columns), BF16),
            vmem((4, rank, columns), BF16),
            vmem((4, rows, columns), F32),
            vmem((4, rows, columns), F32),
            vmem((4, rows, columns), F32),
            vmem((3, rows, columns), BF16),
            vmem((3, rows, columns), BF16),
            vmem((segs, HALF, 128), F32),
            vmem((segs, HALF, 128), BF16),
            vmem((chips - 1, segs, HALF, 128), BF16),
            vmem((2, segs, HALF, 128), BF16),
            vmem((rows, columns), F32),
            dma((14,)),
            dma((3,)),
            dma((3,)),
            dma((6,)),
            dma((6,)),
            dma((2,)),
            dma((2,)),
            dma((2 * len(PIECES),)),
            dma((2 * len(PIECES),)),
            dma((2 * len(PIECES),)),
            dma((2 * len(PIECES),)),
            dma((3,)),
            dma((3,)),
            dma((4,)),
            dma((4,)),
            dma((3,)),
            dma((3,)),
            dma((CHUNKS * chips,)),
            dma((CHUNKS * chips,)),
        ],
        compiler_params=pltpu.CompilerParams(
            collective_id=0, has_side_effects=True, vmem_limit_bytes=63 * 1024 * 1024
        ),
        cost_estimate=pl.CostEstimate(flops=2_000_000_000, bytes_accessed=4_500_000, transcendentals=0),
    )(tokens.reshape(segs, SEG, width), w, down, up, slot, ids, live)


def solution(mesh):
    placed = (
        P("dp", "tensor"),
        P("tensor", None),
        P("dp", None, "tensor"),
        P("dp", None, "tensor"),
        P(),
        P("dp"),
        P("dp"),
    )
    return jax.shard_map(
        functools.partial(per_device, mesh.shape["dp"], mesh.shape["tensor"]),
        mesh=mesh,
        in_specs=placed,
        out_specs=P("dp", "tensor"),
        check_vma=False,
    )
```

```python
import functools

import jax
import jax.numpy as jnp
from jax import lax
from jax.experimental import pallas as pl
from jax.experimental.pallas import tpu as pltpu
from jax.sharding import PartitionSpec as P

MESH = pl.DeviceIdType.MESH
F32 = jnp.float32
BF16 = jnp.bfloat16

RING = 8
SEG = 128
RANK = 64
HALF = RANK // 2
SHORT = 384
PIECES = ((384, 256), (640, 384))
GROUPS = 128 // HALF
CHUNKS = 3
STEP = 3
ORDER = (2, 1, 3, 0)


def nt_dot(a, b):
    return lax.dot_general(a, b, (((1,), (1,)), ((), ())), preferred_element_type=F32)


def kernel(
    n_dp,
    n_tensor,
    tokens_hbm,
    w_hbm,
    down_hbm,
    up_hbm,
    slot_hbm,
    ids_hbm,
    live_hbm,
    out_ref,
    tok,
    tok_other,
    w,
    down,
    up,
    slot,
    ids,
    live,
    req_out,
    req_in,
    a_out,
    a_in,
    relay,
    b_out,
    b_in,
    mine,
    core_out,
    core_in,
    x_out,
    x_in,
    s_mine,
    s_out,
    s_in,
    s_all,
    acc,
    load_sem,
    req_send,
    req_recv,
    a_send,
    a_recv,
    swap_send,
    swap_recv,
    relay_send,
    relay_recv,
    pass_send,
    pass_recv,
    b_send,
    b_recv,
    core_send,
    core_recv,
    x_send,
    x_recv,
    s_send,
    s_recv,
):
    me = lax.axis_index("dp")
    t = lax.axis_index("tensor")
    n_chip = n_tensor // 2
    segs = tok.shape[0]
    stored = down.shape[0]

    core = lax.rem(t, 2)
    sides = (t, t + 1 - 2 * core)

    def dp_at(offset, cross=0):
        return (lax.rem(me + offset + n_dp, n_dp), sides[cross])

    def tensor_at(offset):
        return (me, lax.rem(t + offset, n_tensor))

    other_core = (me, sides[1])

    def far_relay(asker):
        return asker // RING * RING + lax.rem(lax.rem(asker, RING) + 5, RING)

    relay_to = (far_relay(lax.rem(me + n_dp - 3, n_dp)), t)
    pass_index = me // RING * RING + lax.rem(lax.rem(me, RING) + RING - 5, RING)
    pass_to = [(pass_index, side) for side in sides]

    def remote(src, dst, send, recv, device):
        return pltpu.make_async_remote_copy(
            src_ref=src, dst_ref=dst, send_sem=send, recv_sem=recv, device_id=device, device_id_type=MESH
        )

    barrier = pltpu.get_barrier_semaphore()
    peers = [dp_at(o) for o in (-1, -2, -3)] + [pass_to[0]]
    peers += [tensor_at(k) for k in range(1, n_tensor)]
    for peer in peers:
        pl.semaphore_signal(barrier, inc=1, device_id=peer, device_id_type=MESH)

    small = [
        pltpu.make_async_copy(src, dst, load_sem.at[i])
        for i, (src, dst) in enumerate(((slot_hbm, slot), (ids_hbm, ids), (live_hbm, live)))
    ]
    down_load = pltpu.make_async_copy(down_hbm, down, load_sem.at[3])
    up_load = pltpu.make_async_copy(up_hbm, up, load_sem.at[4])
    tok_load = pltpu.make_async_copy(tokens_hbm, tok, load_sem.at[5])
    w_load = []
    for i, k in enumerate(ORDER):
        for side in range(2):
            owner = lax.rem(t + 2 * k, n_tensor)
            if side:
                owner = owner + 1 - 2 * lax.rem(owner, 2)
            columns = pl.ds(pl.multiple_of(owner * 128, 128), 128)
            w_load.append(
                pltpu.make_async_copy(
                    w_hbm.at[:, columns], w.at[i, :, pl.ds(side * 128, 128)], load_sem.at[6 + 2 * i + side]
                )
            )
    for copy in small:
        copy.start()
    down_load.start()
    tok_load.start()
    for copy in w_load:
        copy.start()
    up_load.start()

    for copy in small:
        copy.wait()
    offs, locs = [], []
    for s in range(segs):
        place = slot[ids[s]]
        offs.append(lax.rem(place // stored - me + n_dp, n_dp))
        locs.append(lax.rem(place, stored))
    wanted = []
    for o in range(4):
        found = jnp.int32(0)
        for s in range(4):
            found = jnp.where(offs[s] == o, locs[s], found)
        wanted.append(found)
    far_seg = jnp.int32(0)
    for s in range(4):
        far_seg = jnp.where(offs[s] == 3, s, far_seg)
    live_count = live[0]
    for o in range(1, 4):
        req_out[o - 1] = jnp.full(req_out.shape[1:], wanted[o], jnp.int32)

    pl.semaphore_wait(barrier, len(peers))
    asks = [
        remote(req_out.at[o - 1], req_in.at[o - 1], req_send.at[o - 1], req_recv.at[o - 1], dp_at(o))
        for o in range(1, 4)
    ]
    for copy in asks:
        copy.start()

    core_copies, swap_copies, s_copies = [], [], []

    def rank_half(cross):
        start_row = (1 - core) * HALF if cross else core * HALF
        return pl.ds(pl.multiple_of(start_row, HALF), HALF)

    x_copies = [
        remote(x_out.at[i], x_in.at[i], x_send.at[i], x_recv.at[i], tensor_at(2 * ORDER[i])) for i in range(3)
    ]
    a_copies, b_copies, relay_copies, pass_copies = [], [], [], []
    for o in range(1, 4):
        for cross in range(2):
            lanes = pl.ds(0, a_out.shape[2] if o < 3 else SHORT)
            n = 2 * (o - 1) + cross
            src = a_out.at[o, rank_half(cross), lanes]
            a_copies.append(remote(src, a_in.at[o, cross, :, lanes], a_send.at[n], a_recv.at[n], dp_at(-o, cross)))
        b_copies.append(remote(b_out.at[o - 1], b_in.at[o], b_send.at[o - 1], b_recv.at[o - 1], dp_at(-o)))
    for p, (first, size) in enumerate(PIECES):
        for cross in range(2):
            n = 2 * p + cross
            src = a_out.at[3, rank_half(cross), pl.ds(first, size)]
            here = relay.at[cross, :, pl.ds(first - SHORT, size)]
            dst = a_in.at[3, cross, :, pl.ds(first, size)]
            relay_copies.append(remote(src, here, relay_send.at[n], relay_recv.at[n], relay_to))
            pass_copies.append(remote(here, dst, pass_send.at[n], pass_recv.at[n], pass_to[cross]))

    def base_block(i):
        w_load[2 * i].wait()
        w_load[2 * i + 1].wait()
        for s in range(0, segs, STEP):
            rows = tok[pl.ds(s, STEP)].reshape(STEP * SEG, tok.shape[2])
            part = jnp.dot(rows, w[i], preferred_element_type=F32)
            mine[i, pl.ds(s * SEG, STEP * SEG), :] = part[:, :128]
            core_out[i, pl.ds(s * SEG, STEP * SEG), :] = part[:, 128:]
        copy = remote(core_out.at[i], core_in.at[i], core_send.at[i], core_recv.at[i], other_core)
        copy.start()
        core_copies.append(copy)

    def base_send(i):
        core_copies[i].wait_recv()
        x_out[i] = (mine[i] + core_in[i]).astype(BF16)
        x_copies[i].start()

    def pick(o):
        asks[o - 1].wait_recv()
        asked = jnp.max(req_in[o - 1])
        a_out[o] = down[asked]
        b_out[o - 1] = up[asked]

    def give(o, *crosses):
        for cross in crosses:
            a_copies[2 * (o - 1) + cross].start()

    def pass_on():
        for there, onward in zip(relay_copies, pass_copies):
            there.wait_recv()
            onward.start()

    def serve(near):
        late = range(near + 1, 4)
        for o in late:
            pick(o)
            if o < 3:
                give(o, 0)
        for copy in relay_copies:
            copy.start()
        give(3, 0, 1)
        for o in reversed(late):
            if o < 3:
                give(o, 1)
        for o in late:
            b_copies[o - 1].start()

    def serve_all():
        pick(1)
        give(1, 0)
        base_send(0)
        pick(2)
        give(2, 0)
        pick(3)
        for copy in relay_copies:
            copy.start()
        give(3, 0, 1)
        give(2, 1)
        give(1, 1)
        for copy in b_copies:
            copy.start()
        base_send(1)
        base_send(2)
        swap()
        pass_on()

    def serve_within(near):
        base_send(0)
        for o in range(1, 1 + near):
            pick(o)
            give(o, 0, 1)
            b_copies[o - 1].start()
        base_send(1)
        base_send(2)
        swap()
        pass_on()
        serve(near)

    def swap():
        for copy in swap_copies:
            copy.start()

    tok_load.wait()
    base_block(0)
    base_block(1)
    down_load.wait()
    up_load.wait()
    a_out[0] = down[wanted[0]]
    a_in[0, 0] = a_out[0, rank_half(0)]
    b_in[0] = up[wanted[0]]
    base_block(2)
    base_block(3)
    swap_copies.append(remote(tok, tok_other, swap_send.at[0], swap_recv.at[0], other_core))
    swap_copies.append(remote(a_out.at[0, rank_half(1)], a_in.at[0, 1], swap_send.at[1], swap_recv.at[1], other_core))

    @pl.when(me > 2)
    def _():
        serve_all()

    for near in range(3):

        @pl.when(me == near)
        def _():
            serve_within(near)

    lane_group = lax.broadcasted_iota(jnp.int32, (SEG, 128), 1) // HALF
    row_group = lax.broadcasted_iota(jnp.int32, (SEG, 128), 0) // HALF
    own_group = lane_group == row_group

    def spread(a):
        return jnp.concatenate([a] * GROUPS, axis=0)

    for copy in swap_copies + a_copies + pass_copies:
        copy.wait_recv()
    chunk = segs // CHUNKS
    parts = [pl.ds(h * chunk, chunk) for h in range(CHUNKS)]
    sums = [[] for _ in parts]
    for h, part in enumerate(parts):
        for s in range(h * chunk, (h + 1) * chunk):
            o = jnp.minimum(offs[s], 3)
            both = nt_dot(tok[s], spread(a_in[o, 0])) + nt_dot(tok_other[s], spread(a_in[o, 1]))
            kept = jnp.where(own_group, both, 0.0)
            packed = kept[:HALF]
            for g in range(1, GROUPS):
                packed = packed + kept[g * HALF : (g + 1) * HALF]
            s_mine[s] = packed
            s_out[s] = packed.astype(BF16)
        for k in ORDER[:3]:
            n = h * n_chip + k
            copy = remote(s_out.at[part], s_in.at[k - 1, part], s_send.at[n], s_recv.at[n], tensor_at(2 * k))
            copy.start()
            sums[h].append(copy)

    core_copies[3].wait_recv()
    for copy in x_copies:
        copy.wait_recv()
    acc[...] = mine[3] + core_in[3] + x_in[0].astype(F32) + x_in[1].astype(F32) + x_in[2].astype(F32)

    for h, part in enumerate(parts):
        for copy in sums[h]:
            copy.wait_recv()
        total = s_mine[part]
        for k in range(n_chip - 1):
            total = total + s_in[k, part].astype(F32)
        s_all[core, part] = total.astype(BF16)
        mine_part = s_all.at[core, part]
        copy = remote(mine_part, mine_part, s_send.at[h * n_chip], s_recv.at[h * n_chip], other_core)
        copy.start()
        s_copies.append(copy)

    for copy in b_copies:
        copy.wait_recv()
    for s in range(segs):
        if s % chunk == 0:
            s_copies[s // chunk].wait_recv()
        factor = b_in[jnp.minimum(offs[s], 3)]
        add = None
        for h in range(2):
            x = jnp.where(own_group, spread(s_all[h, s].astype(F32)), 0.0).astype(BF16)
            term = jnp.dot(x, spread(factor[h * HALF : (h + 1) * HALF]), preferred_element_type=F32)
            add = term if add is None else add + term
        add = jnp.where(s < live_count, add, 0.0)
        rows = pl.ds(s * SEG, SEG)
        out_ref[rows, :] = (acc[rows, :] + add).astype(out_ref.dtype)

    for copy in asks + a_copies + swap_copies + relay_copies + pass_copies + b_copies + core_copies + x_copies + s_copies + sum(sums, []):
        copy.wait_send()


def per_device(n_dp, n_tensor, tokens, w, down, up, slot, ids, live):
    rows, width = tokens.shape
    segs = ids.shape[0]
    stored, rank, columns = up.shape
    chips = n_tensor // 2
    dma = pltpu.SemaphoreType.DMA
    vmem, smem = pltpu.VMEM, pltpu.SMEM
    return pl.pallas_call(
        functools.partial(kernel, n_dp, n_tensor),
        name="adapted_projection",
        out_shape=pltpu.VMEM((rows, columns), BF16),
        in_specs=[pl.BlockSpec(memory_space=pl.ANY)] * 7,
        out_specs=pl.BlockSpec(memory_space=pltpu.VMEM),
        scratch_shapes=[
            vmem((segs, SEG, width), BF16),
            vmem((segs, SEG, width), BF16),
            vmem((4, width, 2 * columns), BF16),
            vmem((stored, rank, width), BF16),
            vmem((stored, rank, columns), BF16),
            smem(slot.shape, jnp.int32),
            smem(ids.shape, jnp.int32),
            smem(live.shape, jnp.int32),
            vmem((3, 8, 128), jnp.int32),
            vmem((3, 8, 128), jnp.int32),
            vmem((4, rank, width), BF16),
            vmem((4, 2, HALF, width), BF16),
            vmem((2, HALF, width - SHORT), BF16),
            vmem((3, rank, columns), BF16),
            vmem((4, rank, columns), BF16),
            vmem((4, rows, columns), F32),
            vmem((4, rows, columns), F32),
            vmem((4, rows, columns), F32),
            vmem((3, rows, columns), BF16),
            vmem((3, rows, columns), BF16),
            vmem((segs, HALF, 128), F32),
            vmem((segs, HALF, 128), BF16),
            vmem((chips - 1, segs, HALF, 128), BF16),
            vmem((2, segs, HALF, 128), BF16),
            vmem((rows, columns), F32),
            dma((14,)),
            dma((3,)),
            dma((3,)),
            dma((6,)),
            dma((6,)),
            dma((2,)),
            dma((2,)),
            dma((2 * len(PIECES),)),
            dma((2 * len(PIECES),)),
            dma((2 * len(PIECES),)),
            dma((2 * len(PIECES),)),
            dma((3,)),
            dma((3,)),
            dma((4,)),
            dma((4,)),
            dma((3,)),
            dma((3,)),
            dma((CHUNKS * chips,)),
            dma((CHUNKS * chips,)),
        ],
        compiler_params=pltpu.CompilerParams(
            collective_id=0, has_side_effects=True, vmem_limit_bytes=63 * 1024 * 1024
        ),
        cost_estimate=pl.CostEstimate(flops=2_000_000_000, bytes_accessed=4_500_000, transcendentals=0),
    )(tokens.reshape(segs, SEG, width), w, down, up, slot, ids, live)


def solution(mesh):
    placed = (
        P("dp", "tensor"),
        P("tensor", None),
        P("dp", None, "tensor"),
        P("dp", None, "tensor"),
        P(),
        P("dp"),
        P("dp"),
    )
    return jax.shard_map(
        functools.partial(per_device, mesh.shape["dp"], mesh.shape["tensor"]),
        mesh=mesh,
        in_specs=placed,
        out_specs=P("dp", "tensor"),
        check_vma=False,
    )
```
